512 devices in a mesh: row: 32 (over y_lo, x, core), col: 16 (over z, y_hi).
Axes of the slice: x: 4, y: 8 (y_hi: 2, y_lo: 4; y = y_hi * 4 + y_lo), z: 8, core: 2. Of those that a mesh axis runs over, the one named last changes fastest.
Arguments:
- features: bfloat16 [256, 256, 384], P('row', 'col'), may hold values from -30 to 30
- w_query: bfloat16 [384, 384], replicated, may hold values from -0.3125 to 0.3125
- w_key: bfloat16 [384, 384], replicated, may hold values from -0.3125 to 0.3125
- w_value: bfloat16 [384, 384], replicated, may hold values from -0.3125 to 0.3125
- w_out: bfloat16 [384, 384], replicated, may hold values from -0.625 to 0.625
- logit_scale: float32 [6], replicated, may hold values from 2 to 16
- dw_kernel: float32 [49, 384], replicated, may hold values from -2 to 2
- dw_bias: float32 [384], replicated, may hold values from -3 to 3
- ln_gain: float32 [384], replicated, may hold values from 0.5 to 1.5
- ln_bias: float32 [384], replicated, may hold values from -2 to 2
- w_up: bfloat16 [384, 1280], replicated, may hold values from -0.3125 to 0.3125
- b_up: float32 [1280], replicated, may hold values from -3 to 3
- w_down: bfloat16 [1280, 384], replicated, may hold values from -0.15625 to 0.15625
- b_down: float32 [384], replicated, may hold values from -3 to 3
- layer_scale: float32 [384], replicated, may hold values from 0.5 to 1.5
- cotangent: bfloat16 [256, 256, 384], P('row', 'col'), may hold values from -6 to 6
- tile_list: int32 [32, 16, 8], P('row', 'col'), may hold values from -1 to 7, as said below
Outputs:
- output: bfloat16 [256, 256, 384], P('row', 'col')
- grad_mixed: float32 [256, 256, 384], P('row', 'col')
- grad_w_up: float32 [491520], P(('row', 'col'))
- grad_w_down: float32 [491520], P(('row', 'col'))
- grad_dw_kernel: float32 [49, 384], replicated
- grad_dw_bias: float32 [384], replicated
- grad_ln_gain: float32 [384], replicated
- grad_ln_bias: float32 [384], replicated
- grad_b_up: float32 [1280], replicated
- grad_b_down: float32 [384], replicated
- grad_layer_scale: float32 [384], replicated
The draws below stay inside these ranges and needn't reach their ends.
Inputs may be any that keep to these rules, and one draw needn't show every extreme that they name: `tile_list`: each device's list names its occupied tiles in increasing order, then -1 to the end. A device and the device whose col index differs by 8 hold exactly 10 occupied tiles together; some device holds all 8.
All inputs are finite; a program needn't handle non-finite values.
Results may differ from the reference program's by a relative error of at most 0.0095.
Values may be sent and summed in bfloat16 or wider, within the bound.
No kernel may reach another device: no remote copies, remote signals or barrier semaphores. Data moves between devices by JAX's collectives and lax.ppermute only.
A program may use at most 64 MiB of HBM per device.

```python
import math
import jax
import jax.numpy as jnp
from jax import lax

C = 384
HID = 1280
HEADS = 6
HDIM = 64
POOL = 8
TS = 4
HB = 8
WB = 16
TILES = 8
NH = 256
NW = 256
N_ROW = 32
N_COL = 16


def draw_features(key, part):
    key = jax.random.fold_in(key, 23)
    pixel_key, channel_key, base_key = jax.random.split(key, 3)
    pixel_scale = jnp.exp(jax.random.uniform(pixel_key, (NH, NW, 1), jnp.float32, -1.15, 1.15))
    channel_scale = jnp.exp(jax.random.uniform(channel_key, (C,), jnp.float32, -0.7, 0.7))
    base = jnp.clip(jax.random.normal(base_key, (NH, NW, C), jnp.float32), -4.0, 4.0)
    return (base * pixel_scale * channel_scale).astype(jnp.bfloat16)


def draw_dw_kernel(key, part):
    key = jax.random.fold_in(key, 37)
    base_key, channel_key = jax.random.split(key)
    channel_scale = jnp.exp(jax.random.uniform(channel_key, (C,), jnp.float32, -1.2, 1.2))
    base = jnp.clip(jax.random.normal(base_key, (49, C), jnp.float32), -4.0, 4.0)
    return (base * channel_scale / 7.0).astype(jnp.float32)


def shuffled(subkey):
    return jax.random.permutation(subkey, TILES)


def draw_tile_list(key, part):
    key = jax.random.fold_in(key, 11)
    count_key, order_key = jax.random.split(key)
    pair_total = TILES * 5 // 4
    leading = jax.random.randint(count_key, (N_ROW, N_COL // 2), pair_total - TILES, TILES + 1, dtype=jnp.int32)
    leading = leading.at[0, 0].set(TILES)
    counts = jnp.concatenate([leading, pair_total - leading], axis=1)
    ranking = jax.vmap(shuffled)(jax.random.split(order_key, N_ROW * N_COL)).reshape(N_ROW, N_COL, TILES)
    occupied = (ranking < counts[..., None]).astype(jnp.int32)
    ordering = jnp.argsort(1 - occupied, axis=-1, stable=True).astype(jnp.int32)
    position = jnp.arange(TILES, dtype=jnp.int32)
    return jnp.where(position < counts[..., None], ordering, -1).astype(jnp.int32)


def block_scale(key, shape, shards, smallest, high):
    def one(axis_at, blocks):
        draws = jax.random.uniform(jax.random.fold_in(jax.random.fold_in(key, 6), axis_at), (blocks,), jnp.float32, smallest / len(shards), high / len(shards))
        return jnp.repeat(jnp.exp(draws), shape[axis_at] // blocks).reshape((-1,) + (1,) * (len(shape) - axis_at - 1))

    gain = one(*shards[0])
    for cut in shards[1:]:
        gain = gain * one(*cut)
    return gain


def gaussian(own_key, shape, width, limit, cuts=(), kind=jnp.bfloat16):
    values = jax.random.normal(own_key, shape, jnp.float32) * width
    if len(cuts) > 0:
        values = block_scale(own_key, shape, cuts, -0.22, 0.18) * values
    return jnp.clip(values, min=-limit, max=limit).astype(kind)


def setup_inputs(seed: int = 0) -> dict:
    seeds = jax.random.split(jax.random.key(seed), 18)
    return {
        "features": draw_features(jax.random.fold_in(seeds[17], 71), 0),
        "w_query": gaussian(seeds[1], (C, C), C ** -0.5, 0.3125),
        "w_key": gaussian(seeds[2], (C, C), C ** -0.5, 0.3125),
        "w_value": gaussian(seeds[3], (C, C), C ** -0.5, 0.3125),
        "w_out": gaussian(seeds[4], (C, C), (C // 4) ** -0.5, 0.625),
        "logit_scale": jnp.clip(jnp.exp(jax.random.uniform(seeds[5], (HEADS,), jnp.float32, math.log(2.0), math.log(16.0))), 2.0, 16.0),
        "dw_kernel": draw_dw_kernel(jax.random.fold_in(seeds[17], 71), 0),
        "dw_bias": gaussian(seeds[7], (C,), 0.5, 3.0, (), jnp.float32),
        "ln_gain": jnp.clip(1.0 + 0.1 * jax.random.normal(seeds[8], (C,), jnp.float32), 0.5, 1.5),
        "ln_bias": gaussian(seeds[9], (C,), 0.3, 2.0, (), jnp.float32),
        "w_up": gaussian(seeds[10], (C, HID), C ** -0.5, 0.3125),
        "b_up": gaussian(seeds[11], (HID,), 0.5, 3.0, (), jnp.float32),
        "w_down": gaussian(seeds[12], (HID, C), HID ** -0.5, 0.15625),
        "b_down": gaussian(seeds[13], (C,), 0.5, 3.0, (), jnp.float32),
        "layer_scale": jnp.clip(jax.random.uniform(seeds[14], (C,), jnp.float32, 0.5, 1.5), 0.5, 1.5),
        "cotangent": gaussian(seeds[15], (NH, NW, C), 1.0, 6.0, ((0, 32), (1, 16))),
        "tile_list": draw_tile_list(jax.random.fold_in(seeds[17], 71), 0),
    }


EPS_NORM = 1e-06
GELU_SCALE = 0.7978845608028654

def gelu_parts(preact):
    cubic = 0.044715 * preact * preact
    tanh_val = jnp.tanh(GELU_SCALE * preact * (1.0 + cubic))
    value = 0.5 * preact * (1.0 + tanh_val)
    slope = 0.5 * (1.0 + tanh_val) + 0.5 * preact * (1.0 - tanh_val * tanh_val) * GELU_SCALE * (1.0 + 3.0 * cubic)
    return (value, slope)

def head_normed(values, heads):
    shaped = values.reshape(values.shape[:-1] + (heads, values.shape[-1] // heads))
    squares = lax.optimization_barrier(jnp.sum(shaped * shaped, axis=-1, keepdims=True))
    return (shaped / jnp.sqrt(squares + EPS_NORM)).reshape(values.shape)

def sublayer(spatial, cotan, weight, ln_gain, ln_bias, w_up, b_up, w_down, b_down, layer_scale):
    center = spatial - lax.optimization_barrier(jnp.mean(spatial, axis=-1, keepdims=True))
    inv_std = lax.rsqrt(lax.optimization_barrier(jnp.mean(center * center, axis=-1, keepdims=True)) + EPS_NORM)
    standard = center * inv_std
    lnout = (standard * ln_gain + ln_bias).astype(jnp.bfloat16)
    preact = jnp.dot(lnout, w_up, preferred_element_type=jnp.float32) + b_up
    hid_val, slope = gelu_parts(preact)
    hidden = hid_val.astype(jnp.bfloat16)
    branch = (jnp.dot(hidden, w_down, preferred_element_type=jnp.float32) + b_down) * weight
    d_branch = cotan * layer_scale * weight
    d_branch_b = d_branch.astype(jnp.bfloat16)
    d_hidden = lax.dot_general(d_branch_b, w_down, (((1,), (1,)), ((), ())), preferred_element_type=jnp.float32)
    d_pre = d_hidden * slope
    d_pre_b = d_pre.astype(jnp.bfloat16)
    d_lnout = lax.dot_general(d_pre_b, w_up, (((1,), (1,)), ((), ())), preferred_element_type=jnp.float32)
    scaled = d_lnout * ln_gain
    d_spatial = inv_std * (scaled - lax.optimization_barrier(jnp.mean(scaled, axis=-1, keepdims=True)) - standard * lax.optimization_barrier(jnp.mean(scaled * standard, axis=-1, keepdims=True)))
    grad_up = lax.dot_general(lnout, d_pre_b, (((0,), (0,)), ((), ())), preferred_element_type=jnp.float32)
    grad_down = lax.dot_general(hidden, d_branch_b, (((0,), (0,)), ((), ())), preferred_element_type=jnp.float32)
    smalls = (lax.optimization_barrier(jnp.sum(d_lnout * standard, axis=0)), lax.optimization_barrier(jnp.sum(d_lnout, axis=0)), lax.optimization_barrier(jnp.sum(d_pre, axis=0)), lax.optimization_barrier(jnp.sum(d_branch, axis=0)), lax.optimization_barrier(jnp.sum(cotan * branch, axis=0)))
    return (branch, d_spatial, grad_up, grad_down, smalls)

def reference(features, w_query, w_key, w_value, w_out, logit_scale, dw_kernel, dw_bias, ln_gain, ln_bias, w_up, b_up, w_down, b_down, layer_scale, cotangent, tile_list):
    pooled = lax.optimization_barrier(jnp.mean(features.reshape(NH // POOL, POOL, NW, C).astype(jnp.float32), axis=1)).astype(jnp.bfloat16)
    flat_pool = pooled.reshape(-1, C)
    keys = head_normed(jnp.dot(flat_pool, w_key, preferred_element_type=jnp.float32), HEADS).astype(jnp.bfloat16)
    keys = lax.optimization_barrier(keys).astype(jnp.float32).reshape(NH // POOL, NW, HEADS, HDIM)
    values = jnp.dot(flat_pool, w_value, preferred_element_type=jnp.float32).astype(jnp.bfloat16)
    values = lax.optimization_barrier(values).astype(jnp.float32).reshape(NH // POOL, NW, HEADS, HDIM)

    def attend_band(band):
        rows = lax.dynamic_slice_in_dim(features, band * HB, HB, 0)
        query = head_normed(jnp.dot(rows.reshape(-1, C), w_query, preferred_element_type=jnp.float32), HEADS)
        query = lax.optimization_barrier(query.astype(jnp.bfloat16)).astype(jnp.float32).reshape(HB, NW, HEADS, HDIM)
        scores = jnp.einsum('iwhd,jwhd->iwhj', query, keys) * logit_scale[:, None]
        weight = jnp.exp(scores)
        total = lax.optimization_barrier(jnp.sum(weight, axis=-1))
        weight_b = lax.optimization_barrier(weight.astype(jnp.bfloat16)).astype(jnp.float32)
        numer = jnp.einsum('iwhj,jwhd->iwhd', weight_b, values)
        attended = (numer / total[..., None]).astype(jnp.bfloat16).reshape(-1, C)
        mixed_band = rows.reshape(-1, C).astype(jnp.float32) + jnp.dot(attended, w_out, preferred_element_type=jnp.float32)
        return mixed_band.astype(jnp.bfloat16).reshape(HB, NW, C)
    mixed = lax.map(attend_band, jnp.arange(N_ROW, dtype=jnp.int32)).reshape(NH, NW, C)
    hits = jnp.any(tile_list[..., :, None] == jnp.arange(TILES, dtype=jnp.int32), axis=-2).astype(jnp.float32)
    tile_rows = HB // TS
    tile_cols = WB // TS
    occupancy = jnp.broadcast_to(hits.reshape(N_ROW, N_COL, tile_rows, 1, tile_cols, 1), (N_ROW, N_COL, tile_rows, TS, tile_cols, TS))
    occupancy = occupancy.transpose(0, 2, 3, 1, 4, 5).reshape(NH, NW)
    padded = jnp.pad(mixed, ((3, 3), (3, 3), (0, 0)))

    def forward_band(carry, band):
        window = lax.dynamic_slice_in_dim(padded, band * HB, HB + 6, 0)
        spatial = jnp.broadcast_to(dw_bias, (HB, NW, C)).astype(jnp.float32)
        for row_off in range(7):
            for col_off in range(7):
                spatial = spatial + window[row_off:row_off + HB, col_off:col_off + NW].astype(jnp.float32) * dw_kernel[7 * row_off + col_off]
        cotan = lax.dynamic_slice_in_dim(cotangent, band * HB, HB, 0).astype(jnp.float32).reshape(-1, C)
        weight = lax.dynamic_slice_in_dim(occupancy, band * HB, HB, 0).reshape(-1, 1)
        branch, d_spatial, grad_up, grad_down, smalls = sublayer(spatial.reshape(-1, C), cotan, weight, ln_gain, ln_bias, w_up, b_up, w_down, b_down, layer_scale)
        mixed_band = lax.dynamic_slice_in_dim(mixed, band * HB, HB, 0).astype(jnp.float32)
        out_band = (mixed_band + layer_scale * branch.reshape(HB, NW, C)).astype(jnp.bfloat16)
        d_grid = d_spatial.reshape(HB, NW, C)
        taps = []
        for row_off in range(7):
            for col_off in range(7):
                taps.append(lax.optimization_barrier(jnp.sum(d_grid * window[row_off:row_off + HB, col_off:col_off + NW].astype(jnp.float32), axis=(0, 1))))
        kernel_grad = jnp.stack(taps, axis=0)
        new_carry = (carry[0] + grad_up, carry[1] + grad_down, carry[2] + kernel_grad, carry[3] + lax.optimization_barrier(jnp.sum(d_grid, axis=(0, 1))), tuple((old + new for old, new in zip(carry[4], smalls))))
        return (new_carry, (out_band, d_grid))
    zeros_c = jnp.zeros((C,), jnp.float32)
    init = (jnp.zeros((C, HID), jnp.float32), jnp.zeros((HID, C), jnp.float32), jnp.zeros((49, C), jnp.float32), zeros_c, (zeros_c, zeros_c, jnp.zeros((HID,), jnp.float32), zeros_c, zeros_c))
    carry, (out_bands, d_bands) = lax.scan(forward_band, init, jnp.arange(N_ROW, dtype=jnp.int32))
    output = out_bands.reshape(NH, NW, C)
    padded_grad = jnp.pad(d_bands.reshape(NH, NW, C), ((3, 3), (3, 3), (0, 0)))

    def backward_band(band):
        window = lax.dynamic_slice_in_dim(padded_grad, band * HB, HB + 6, 0)
        accum = lax.dynamic_slice_in_dim(cotangent, band * HB, HB, 0).astype(jnp.float32)
        for row_off in range(7):
            for col_off in range(7):
                accum = accum + window[6 - row_off:6 - row_off + HB, 6 - col_off:6 - col_off + NW] * dw_kernel[7 * row_off + col_off]
        return accum
    grad_mixed = lax.map(backward_band, jnp.arange(N_ROW, dtype=jnp.int32)).reshape(NH, NW, C)
    grad_up, grad_down, kernel_grad, bias_grad, smalls = carry
    return (output, grad_mixed, grad_up.reshape(-1), grad_down.reshape(-1), kernel_grad, bias_grad, smalls[0], smalls[1], smalls[2], smalls[3], smalls[4])
```

```python
import jax
import jax.numpy as jnp
from jax import lax
from jax.sharding import Mesh, PartitionSpec as P

ROW = ("yl", "x", "c")
COL = ("z", "yh")
YZ = ("yl", "z", "yh")
XC = ("x", "c")

POOL = 8
TS = 4


EPS_NORM = 1e-06
GELU_SCALE = 0.7978845608028654


def extended(array, sides, width):
    for axis, dim in sides:
        size, length = (lax.axis_size(axis), array.shape[dim])
        up = [(i, (i + 1) % size) for i in range(size - 1)]
        down = [(j, i) for i, j in up]
        last = lax.slice_in_dim(array, length - width, length, axis=dim)
        leading = lax.slice_in_dim(array, 0, width, axis=dim)
        before = lax.ppermute(last, axis, up)
        after = lax.ppermute(leading, axis, down)
        array = jnp.concatenate([before, array, after], axis=dim)
    return array


def gelu_parts(preact):
    cubic = 0.044715 * preact * preact
    tanh_val = jnp.tanh(GELU_SCALE * preact * (1.0 + cubic))
    value = 0.5 * preact * (1.0 + tanh_val)
    slope = 0.5 * (1.0 + tanh_val) + 0.5 * preact * (1.0 - tanh_val * tanh_val) * GELU_SCALE * (
        1.0 + 3.0 * cubic
    )
    return (value, slope)


def head_normed(values, heads):
    shaped = values.reshape(values.shape[:-1] + (heads, values.shape[-1] // heads))
    squares = jnp.sum(shaped * shaped, axis=-1, keepdims=True)
    return (shaped / jnp.sqrt(squares + EPS_NORM)).reshape(values.shape)


def sublayer(spatial, cotan, weight, ln_gain, ln_bias, w_up, b_up, w_down, b_down, layer_scale):
    center = spatial - jnp.mean(spatial, axis=-1, keepdims=True)
    inv_std = lax.rsqrt(jnp.mean(center * center, axis=-1, keepdims=True) + EPS_NORM)
    standard = center * inv_std
    lnout = (standard * ln_gain + ln_bias).astype(jnp.bfloat16)
    preact = jnp.dot(lnout, w_up, preferred_element_type=jnp.float32) + b_up
    hid_val, slope = gelu_parts(preact)
    hidden = hid_val.astype(jnp.bfloat16)
    branch = (jnp.dot(hidden, w_down, preferred_element_type=jnp.float32) + b_down) * weight
    d_branch = cotan * layer_scale * weight
    d_branch_b = d_branch.astype(jnp.bfloat16)
    d_hidden = lax.dot_general(
        d_branch_b, w_down, (((1,), (1,)), ((), ())), preferred_element_type=jnp.float32
    )
    d_pre = d_hidden * slope
    d_pre_b = d_pre.astype(jnp.bfloat16)
    d_lnout = lax.dot_general(
        d_pre_b, w_up, (((1,), (1,)), ((), ())), preferred_element_type=jnp.float32
    )
    scaled = d_lnout * ln_gain
    d_spatial = inv_std * (
        scaled
        - jnp.mean(scaled, axis=-1, keepdims=True)
        - standard * jnp.mean(scaled * standard, axis=-1, keepdims=True)
    )
    grad_up = lax.dot_general(
        lnout, d_pre_b, (((0,), (0,)), ((), ())), preferred_element_type=jnp.float32
    )
    grad_down = lax.dot_general(
        hidden, d_branch_b, (((0,), (0,)), ((), ())), preferred_element_type=jnp.float32
    )
    smalls = (
        jnp.sum(d_lnout * standard, axis=0),
        jnp.sum(d_lnout, axis=0),
        jnp.sum(d_pre, axis=0),
        jnp.sum(d_branch, axis=0),
        jnp.sum(cotan * branch, axis=0),
    )
    return (branch, d_spatial, grad_up, grad_down, smalls)


def reduce_all(grad_up, grad_down, smalls):
    n_yl, n_x, n_c = (lax.axis_size(a) for a in ROW)
    n_col = lax.axis_size(COL)
    n_yz = n_yl * n_col
    n_all = n_yz * n_x * n_c
    share = grad_up.size // n_all
    rows = 2 * share // 128
    record = jnp.concatenate(
        [
            grad_up.astype(jnp.bfloat16).reshape(n_all, share),
            grad_down.astype(jnp.bfloat16).reshape(n_all, share),
        ],
        axis=1,
    )
    record = record.reshape(n_yl, n_x, n_c, n_col * rows, 128).transpose(2, 1, 0, 3, 4)
    record = record.reshape(n_c, n_x, n_yz * rows, 128)
    flat = jnp.concatenate([v.reshape(-1) for v in smalls])
    chunk = n_c * n_x * 128
    small_rows = -(-flat.size // chunk)
    small_pad = -(-small_rows // 8) * 8
    flat = jnp.pad(flat, (0, small_rows * chunk - flat.size))
    flat = flat.reshape(n_c, n_x, small_rows, 128)
    flat = jnp.pad(flat, ((0, 0), (0, 0), (0, small_pad - small_rows), (0, 0)))
    both = jnp.concatenate([record, flat.astype(jnp.bfloat16)], axis=2)
    core = lax.axis_index("c")
    other = lax.dynamic_index_in_dim(both, 1 - core, 0, keepdims=False)
    mine = lax.dynamic_index_in_dim(both, core, 0, keepdims=False)
    got = lax.ppermute(other, "c", [(0, 1), (1, 0)])
    part = (mine.astype(jnp.float32) + got.astype(jnp.float32)).astype(jnp.bfloat16)
    part = lax.all_to_all(part, "x", 0, 0, tiled=True)
    part = jnp.sum(part.astype(jnp.float32), axis=0).astype(jnp.bfloat16)
    big = part[: n_yz * rows].reshape(n_yz, rows, 128)
    small = jnp.broadcast_to(part[n_yz * rows :], (n_yz, small_pad, 128))
    part = jnp.concatenate([big, small], axis=1)
    part = lax.all_to_all(part, YZ, 0, 0, tiled=True)
    part = jnp.sum(part.astype(jnp.float32), axis=0)
    share_up = part[:rows].reshape(-1)[:share]
    share_down = part[:rows].reshape(-1)[share:]
    small = jnp.broadcast_to(part[rows:], (n_x * n_c, small_pad, 128))
    small = lax.all_to_all(small, XC, 0, 0, tiled=True)
    small = small[:, :small_rows].reshape(n_x, n_c, -1).transpose(1, 0, 2).reshape(-1)
    outs, at = [], 0
    for v in smalls:
        outs.append(small[at : at + v.size].reshape(v.shape))
        at += v.size
    return share_up, share_down, tuple(outs)


def body(
    features,
    w_query,
    w_key,
    w_value,
    w_out,
    logit_scale,
    dw_kernel,
    dw_bias,
    ln_gain,
    ln_bias,
    w_up,
    b_up,
    w_down,
    b_down,
    layer_scale,
    cotangent,
    tile_list,
):
    rows_here, cols_here, chans = features.shape
    heads = logit_scale.shape[0]
    head_width = chans // heads
    flat_feat = features.reshape(-1, chans)
    query = head_normed(jnp.dot(flat_feat, w_query, preferred_element_type=jnp.float32), heads)
    query = query.astype(jnp.bfloat16).reshape(rows_here, cols_here, heads, head_width)
    pooled = jnp.mean(
        features.reshape(rows_here // POOL, POOL, cols_here, chans), axis=1, dtype=jnp.float32
    )
    n_row = lax.axis_size(ROW)
    pooled = pooled.astype(jnp.bfloat16).reshape(1, cols_here, chans)
    pooled = lax.all_to_all(
        jnp.broadcast_to(pooled, (n_row, cols_here, chans)), ROW, 0, 0, tiled=True
    )
    flat_pool = pooled.reshape(-1, chans)
    keys = head_normed(jnp.dot(flat_pool, w_key, preferred_element_type=jnp.float32), heads)
    key_piece = keys.astype(jnp.bfloat16).reshape(n_row, cols_here, heads, head_width)
    values = jnp.dot(flat_pool, w_value, preferred_element_type=jnp.float32)
    value_piece = values.astype(jnp.bfloat16).reshape(n_row, cols_here, heads, head_width)
    scores = jnp.einsum("iwhd,jwhd->iwhj", query, key_piece, preferred_element_type=jnp.float32)
    weight = jnp.exp(scores * logit_scale[:, None])
    numer = jnp.einsum(
        "iwhj,jwhd->iwhd",
        weight.astype(jnp.bfloat16),
        value_piece,
        preferred_element_type=jnp.float32,
    )
    numer, total = (numer, jnp.sum(weight, axis=-1))
    attended = (numer / total[..., None]).astype(jnp.bfloat16).reshape(-1, chans)
    mixed = flat_feat.astype(jnp.float32) + jnp.dot(
        attended, w_out, preferred_element_type=jnp.float32
    )
    mixed = mixed.astype(jnp.bfloat16).reshape(rows_here, cols_here, chans)
    padded = extended(mixed, ((ROW, 0), (COL, 1)), 3)
    spatial = jnp.broadcast_to(dw_bias, (rows_here, cols_here, chans))
    for row_off in range(7):
        for col_off in range(7):
            spatial = (
                spatial
                + padded[row_off : row_off + rows_here, col_off : col_off + cols_here].astype(
                    jnp.float32
                )
                * dw_kernel[7 * row_off + col_off]
            )
    tile_rows = rows_here // TS
    tile_cols = cols_here // TS
    tiles_here = tile_rows * tile_cols
    listing = tile_list[0, 0]
    hits = jnp.any(
        listing[:, None] == jnp.arange(tiles_here, dtype=jnp.int32)[None, :], axis=0
    ).astype(jnp.float32)
    pixel_mask = jnp.broadcast_to(
        hits.reshape(tile_rows, 1, tile_cols, 1), (tile_rows, TS, tile_cols, TS)
    )
    pixel_mask = pixel_mask.reshape(rows_here, cols_here)
    cot_full = cotangent.astype(jnp.float32)
    branch, d_spatial, grad_up, grad_down, smalls = sublayer(
        spatial.reshape(-1, chans),
        cot_full.reshape(-1, chans),
        pixel_mask.reshape(-1, 1),
        ln_gain,
        ln_bias,
        w_up,
        b_up,
        w_down,
        b_down,
        layer_scale,
    )
    branch_full = branch.reshape(rows_here, cols_here, chans)
    d_full = d_spatial.reshape(rows_here, cols_here, chans)
    output = (mixed.astype(jnp.float32) + layer_scale * branch_full).astype(jnp.bfloat16)
    d_padded = extended(d_full.astype(jnp.bfloat16), ((ROW, 0), (COL, 1)), 3).astype(
        d_full.dtype
    )
    grad_mixed = cot_full
    taps = []
    for row_off in range(7):
        for col_off in range(7):
            grad_mixed = (
                grad_mixed
                + d_padded[
                    6 - row_off : 6 - row_off + rows_here, 6 - col_off : 6 - col_off + cols_here
                ]
                * dw_kernel[7 * row_off + col_off]
            )
            taps.append(
                jnp.sum(
                    d_full
                    * padded[row_off : row_off + rows_here, col_off : col_off + cols_here].astype(
                        jnp.float32
                    ),
                    axis=(0, 1),
                )
            )
    kernel_grad = jnp.stack(taps, axis=0)
    bias_grad = jnp.sum(d_full, axis=(0, 1))
    gain_grad, shift_grad, up_bias_grad, down_bias_grad, scale_grad = smalls
    up_share, down_share, smalls = reduce_all(
        grad_up,
        grad_down,
        (kernel_grad, bias_grad, gain_grad, shift_grad, up_bias_grad, down_bias_grad, scale_grad),
    )
    return (output, grad_mixed, up_share, down_share) + smalls


def solution(mesh):
    mesh = Mesh(mesh.devices.reshape(4, 4, 2, 8, 2), ROW + COL)
    in_specs = (
        P(ROW, COL, None),
        P(),
        P(),
        P(),
        P(),
        P(),
        P(),
        P(),
        P(),
        P(),
        P(),
        P(),
        P(),
        P(),
        P(),
        P(ROW, COL, None),
        P(ROW, COL, None),
    )
    out_specs = (
        P(ROW, COL, None),
        P(ROW, COL, None),
        P(ROW + COL),
        P(ROW + COL),
        P(),
        P(),
        P(),
        P(),
        P(),
        P(),
        P(),
    )
    return jax.shard_map(body, mesh=mesh, in_specs=in_specs, out_specs=out_specs, check_vma=False)
```

```python
import numpy as np
import jax
import jax.numpy as jnp
from jax import lax
from jax.experimental import pallas as pl
from jax.experimental.pallas import tpu as pltpu
from jax.sharding import Mesh, PartitionSpec as P

ROW = ("yl", "x", "c")
COL = ("z", "yh")
YZ = ("yl", "z", "yh")
CX = ("c", "x")

F32 = jnp.float32
BF16 = jnp.bfloat16
EPS_NORM = 1e-06
GELU_SCALE = 0.7978845608028654
TS = 4
HB = 8
WB = 16
PIX = HB * WB
C = 384
HID = 1280
HEADS = 6
TILES_L = C // 128
N_YL, N_X, N_C, N_Z, N_YH = 4, 4, 2, 8, 2
N_ROW = N_YL * N_X * N_C
N_YZ = N_YL * N_Z * N_YH
SHARE = 960
SMALL = 24
REC = 1056
WCOL = 32

UP_TILES = (
    [(0, t) for t in range(8)],
    [(0, 7), (0, 8), (0, 9)] + [(1, t) for t in range(5)],
    [(1, t) for t in range(5, 10)] + [(2, t) for t in range(3)],
    [(2, t) for t in range(2, 10)],
)
DOWN_TILES = (
    [(0, t) for t in range(3)] + [(1, t) for t in range(3)] + [(2, 0), (2, 1)],
    [(2, 1), (2, 2)] + [(3, t) for t in range(3)] + [(4, t) for t in range(3)],
)


def call(kernel, outs, *args, scratch=(), smem=(), flops=0, nbytes=0, trans=0):
    specs = [
        pl.BlockSpec(memory_space=pltpu.SMEM if i in smem else pltpu.VMEM)
        for i in range(len(args))
    ]
    return pl.pallas_call(
        kernel,
        out_shape=[jax.ShapeDtypeStruct(s, d) for s, d in outs],
        in_specs=specs,
        out_specs=[pl.BlockSpec(memory_space=pltpu.VMEM) for _ in outs],
        scratch_shapes=list(scratch),
        compiler_params=pltpu.CompilerParams(vmem_limit_bytes=40 * 1024 * 1024),
        cost_estimate=pl.CostEstimate(flops=flops, bytes_accessed=nbytes, transcendentals=trans),
    )(*args)


def mm(a, b, dims=((1,), (0,))):
    return lax.dot_general(a, b, (dims, ((), ())), preferred_element_type=F32)


def head_scaled(values):
    block = lax.broadcasted_iota(jnp.int32, (C, C), 0) // 64
    same = (block == lax.broadcasted_iota(jnp.int32, (C, C), 1) // 64).astype(F32).astype(BF16)
    squares = values * values
    high = squares.astype(BF16)
    low = (squares - high.astype(F32)).astype(BF16)
    return values * lax.rsqrt(mm(high, same) + mm(low, same) + EPS_NORM)


def pool_kernel(feat, out):
    total = feat[0].astype(F32)
    for r in range(1, HB):
        total = total + feat[r].astype(F32)
    mean = (total * (1.0 / HB)).astype(BF16)
    for i in range(N_ROW):
        out[i] = mean


def query_kernel(feat, w_query, out):
    out[...] = head_scaled(mm(feat[...], w_query[...])).astype(BF16)


def attention_kernel(scale, pooled, query, feat, w_key, w_value, w_out, mixed, first, last):
    rows = pooled[...]
    keys = head_scaled(mm(rows, w_key[...])).astype(BF16)
    values = mm(rows, w_value[...]).astype(BF16)
    n_keys = N_ROW * WB
    same = (
        lax.broadcasted_iota(jnp.int32, (PIX, n_keys), 0) % WB
        == lax.broadcasted_iota(jnp.int32, (PIX, n_keys), 1) % WB
    )
    lower = lax.broadcasted_iota(jnp.int32, (PIX, 128), 1) < 64
    pairs = []
    for pair in range(HEADS // 2):
        lanes = slice(128 * pair, 128 * pair + 128)
        q = query[:, lanes].astype(F32)
        parts = []
        for half in range(2):
            q_half = jnp.where(lower if half == 0 else ~lower, q, 0.0).astype(BF16)
            scores = mm(q_half, keys[:, lanes], ((1,), (1,)))
            weight = jnp.where(same, jnp.exp(scores * scale[2 * pair + half]), 0.0)
            total = jnp.sum(weight, axis=1, keepdims=True)
            parts.append(mm(weight.astype(BF16), values[:, lanes]) / total)
        pairs.append(jnp.where(lower, parts[0], parts[1]).astype(BF16))
    attended = jnp.concatenate(pairs, axis=1)
    out = (feat[...].astype(F32) + mm(attended, w_out[...])).astype(BF16)
    mixed[...] = out
    first[...] = out[: 3 * WB]
    last[...] = out[PIX - 3 * WB :]


def fill_window(win, own, above, below, left, right):
    for r in range(3):
        win[r, 8 : 8 + WB, :] = above[r * WB : (r + 1) * WB, :].astype(F32)
        win[3 + HB + r, 8 : 8 + WB, :] = below[r * WB : (r + 1) * WB, :].astype(F32)
    for r in range(HB):
        win[3 + r, 8 : 8 + WB, :] = own[r * WB : (r + 1) * WB, :].astype(F32)
    lcols = left[...].astype(F32)
    rcols = right[...].astype(F32)
    for r in range(HB + 6):
        win[r, 5:8, :] = lcols[3 * r : 3 * r + 3]
        win[r, 8 + WB : 11 + WB, :] = rcols[3 * r : 3 * r + 3]


def depthwise(win, taps, start, flip, store):
    for t in range(TILES_L):
        lanes = slice(128 * t, 128 * t + 128)
        acc = [start(r, lanes) for r in range(HB)]
        for dj in range(7):
            cols = [win[r, 5 + dj : 5 + dj + WB, lanes] for r in range(HB + 6)]
            for di in range(7):
                tap = 7 * di + dj if not flip else 7 * (6 - di) + (6 - dj)
                k = taps[tap : tap + 1, lanes]
                for r in range(HB):
                    acc[r] = acc[r] + cols[r + di] * k
        for r in range(HB):
            store(r, lanes, acc[r])


def rowsum(a):
    return jnp.sum(a, axis=0, keepdims=True)


def sublayer_kernel(
    own, above, below, left, right, cot, occ, taps, dw_bias, ln_gain, ln_bias,
    w_up, b_up, w_down, b_down, layer_scale,
    output, d_out, d_first, d_last, win_out, lnout_out, hidden_out, d_pre_out, d_branch_out, sums,
    win, spat,
):
    fill_window(win, own, above, below, left, right)
    win_out[...] = win[...].astype(BF16)

    def store(r, lanes, value):
        spat[r * WB : (r + 1) * WB, lanes] = value

    depthwise(
        win, taps, lambda r, lanes: jnp.broadcast_to(dw_bias[:, lanes], (WB, 128)), False, store
    )
    spatial = spat[...]
    center = spatial - jnp.mean(spatial, axis=1, keepdims=True)
    inv_std = lax.rsqrt(jnp.mean(center * center, axis=1, keepdims=True) + EPS_NORM)
    standard = center * inv_std
    gain = ln_gain[...]
    lnout = (standard * gain + ln_bias[...]).astype(BF16)
    lnout_out[...] = lnout
    preact = mm(lnout, w_up[...]) + b_up[...]
    square = 0.044715 * preact * preact
    tanh_val = jnp.tanh(GELU_SCALE * preact * (1.0 + square))
    hidden = (0.5 * preact * (1.0 + tanh_val)).astype(BF16)
    slope = 0.5 * (1.0 + tanh_val) + 0.5 * preact * (1.0 - tanh_val * tanh_val) * GELU_SCALE * (
        1.0 + 3.0 * square
    )
    hidden_out[...] = hidden
    weight = occ[...]
    scale = layer_scale[...]
    cotan = cot[...].astype(F32)
    d_branch = cotan * scale * weight
    d_branch_b = d_branch.astype(BF16)
    d_branch_out[...] = d_branch_b
    d_pre = mm(d_branch_b, w_down[...], ((1,), (1,))) * slope
    d_pre_b = d_pre.astype(BF16)
    d_pre_out[...] = d_pre_b
    d_lnout = mm(d_pre_b, w_up[...], ((1,), (1,)))
    e = d_lnout * gain
    d_spatial = inv_std * (
        e
        - jnp.mean(e, axis=1, keepdims=True)
        - standard * jnp.mean(e * standard, axis=1, keepdims=True)
    )
    d_out[...] = d_spatial
    d_first[...] = d_spatial[: 3 * WB].astype(BF16)
    d_last[...] = d_spatial[PIX - 3 * WB :].astype(BF16)
    branch = (mm(hidden, w_down[...]) + b_down[...]) * weight
    output[...] = (own[...].astype(F32) + scale * branch).astype(BF16)
    sums[0:1, :C] = rowsum(d_spatial)
    sums[1:2, :C] = rowsum(d_lnout * standard)
    sums[2:3, :C] = rowsum(d_lnout)
    sums[3:4, :C] = rowsum(d_branch)
    sums[4:5, :C] = rowsum(cotan * branch)
    sums[5:6, :] = rowsum(d_pre)


def up_order():
    chan = np.arange(C).reshape(N_YL, N_X, N_C, N_Z // 2, 3).transpose(4, 2, 1, 0, 3).reshape(-1)
    return (np.arange(C)[:, None] == chan[None, :]).astype(np.float32)


def gradient_kernel(
    core, order, lnout, hidden, d_pre, d_branch, win_in, d_spatial, sums, mine, other, win, down, small
):
    is_zero = core[0] == 0

    def put(row, x, zero, one):
        size = zero.shape[0]
        mine[x, row : row + size, :] = jnp.where(is_zero, zero, one).astype(BF16)
        other[x, row : row + size, :] = jnp.where(is_zero, one, zero).astype(BF16)

    ordered = mm(lnout[...], order[...]).astype(BF16)
    ups = [mm(ordered[:, 128 * r : 128 * r + 128], d_pre[...], ((0,), (0,))) for r in range(3)]
    for q in range(4):
        for k, (r, t) in enumerate(UP_TILES[q]):
            for x in range(N_X):
                pair = [ups[r][64 * c + 16 * x : 64 * c + 16 * x + 16, 128 * t : 128 * t + 128] for c in range(2)]
                put((q * 8 + k) * 16, x, *pair)
    full = mm(hidden[...], d_branch[...], ((0,), (0,)))
    for t in range(TILES_L):
        down[t] = full[:, 128 * t : 128 * t + 128]
    for yh in range(2):
        for k, (s, t) in enumerate(DOWN_TILES[yh]):
            for x in range(N_X):
                for two in range(2):
                    pair = [
                        jnp.concatenate(
                            [
                                down[t, pl.ds(5 * (64 * yl + 16 * x + 8 * c) + s, 8, stride=5), :]
                                for yl in (2 * two, 2 * two + 1)
                            ],
                            axis=0,
                        )
                        for c in range(2)
                    ]
                    put(512 + (yh * 8 + k) * 32 + 16 * two, x, *pair)
    win[...] = win_in[...].astype(F32)
    small[...] = jnp.zeros_like(small)
    for t in range(TILES_L):
        lanes = slice(128 * t, 128 * t + 128)
        d_rows = [d_spatial[r * WB : (r + 1) * WB, lanes] for r in range(HB)]
        for dj in range(7):
            cols = [win[r, 5 + dj : 5 + dj + WB, lanes] for r in range(HB + 6)]
            for di in range(7):
                acc = cols[di] * d_rows[0]
                for r in range(1, HB):
                    acc = acc + cols[r + di] * d_rows[r]
                at = 56 * t + 7 * di + dj
                small[at : at + 1, :] = rowsum(acc)
    for i in range(5):
        for t in range(TILES_L):
            small[161 + 3 * i + t : 162 + 3 * i + t, :] = sums[i : i + 1, 128 * t : 128 * t + 128]
    for t in range(HID // 128):
        small[176 + t : 177 + t, :] = sums[5:6, 128 * t : 128 * t + 128]
    for x in range(N_X):
        pair = [
            jnp.concatenate([small[96 * c + 24 * x : 96 * c + 24 * x + 24], jnp.zeros((8, 128), F32)], axis=0)
            for c in range(2)
        ]
        put(1024, x, *pair)


def spread_kernel(part, out, total):
    total[...] = (
        (part[0].astype(F32) + part[1].astype(F32)) + (part[2].astype(F32) + part[3].astype(F32))
    )
    small = total[1024 : 1024 + SMALL, :]
    for yl in range(N_YL):
        for z in range(N_Z):
            for yh in range(N_YH):
                q = (z % 2) * 2 + yh
                up = total[pl.ds(q * 128 + yl * 4 + z // 2, 8, stride=16), :]
                down = total[pl.ds(512 + yh * 256 + yl * 8 + z, 8, stride=32), :]
                record = jnp.concatenate([up, down, small], axis=0)
                out[(yl * N_Z + z) * N_YH + yh] = record.astype(BF16)


def gather_kernel(part, share, small):
    total = part[0].astype(F32)
    for i in range(1, N_YZ):
        total = total + part[i].astype(F32)
    share[...] = total[:16]
    for i in range(N_X * N_C):
        small[i] = total[16:]


def final_kernel(small, dw, *vectors):
    for t in range(TILES_L):
        dw[:, 128 * t : 128 * t + 128] = small[56 * t : 56 * t + 49, :]
    for i in range(5):
        for t in range(TILES_L):
            vectors[i][:, 128 * t : 128 * t + 128] = small[161 + 3 * i + t : 162 + 3 * i + t, :]
    for t in range(HID // 128):
        vectors[5][:, 128 * t : 128 * t + 128] = small[176 + t : 177 + t, :]


def spread_grad_kernel(own, above, below, left, right, cot, taps, out, win):
    fill_window(win, own, above, below, left, right)

    def store(r, lanes, value):
        out[r * WB : (r + 1) * WB, lanes] = value

    depthwise(
        win, taps, lambda r, lanes: cot[r * WB : (r + 1) * WB, lanes].astype(F32), True, store
    )


def core_sum_kernel(mine, got, first, last, out):
    out[...] = (mine[...].astype(F32) + got[...].astype(F32)).astype(BF16)


def neighbours(before_edge, after_edge, axes):
    size = lax.axis_size(axes)
    up = [(i, i + 1) for i in range(size - 1)]
    down = [(i + 1, i) for i in range(size - 1)]
    return lax.ppermute(after_edge, axes, up), lax.ppermute(before_edge, axes, down)


def column_edges(own, above, below):
    rows = jnp.concatenate([above, own, below], axis=0).reshape(HB + 6, WB, C)
    return rows[:, :3].reshape(-1, C), rows[:, WB - 3 :].reshape(-1, C)


def body(
    features, w_query, w_key, w_value, w_out, logit_scale, dw_kernel, dw_bias, ln_gain, ln_bias,
    w_up, b_up, w_down, b_down, layer_scale, cotangent, tile_list,
):
    row = lambda v: v.reshape(1, -1)
    flat = features.reshape(PIX, C)
    cot = cotangent.reshape(PIX, C)

    (copies,) = call(pool_kernel, [((N_ROW, WB, C), BF16)], features, nbytes=500_000)
    pooled = lax.all_to_all(copies, ROW, 0, 0, tiled=True).reshape(N_ROW * WB, C)
    (query,) = call(query_kernel, [((PIX, C), BF16)], flat, w_query, flops=10**8, nbytes=500_000)
    tiles = jnp.arange(HB // TS * (WB // TS), dtype=jnp.int32)
    hits = jnp.any(tile_list[0, 0][:, None] == tiles[None, :], axis=0).astype(F32)
    occ = jnp.broadcast_to(hits.reshape(HB // TS, 1, WB // TS, 1), (HB // TS, TS, WB // TS, TS))
    occ = occ.reshape(PIX, 1)

    edge = ((3 * WB, C), BF16)
    mixed, first, last = call(
        attention_kernel, [((PIX, C), BF16), edge, edge],
        logit_scale, pooled, query, flat, w_key, w_value, w_out,
        smem=(0,), flops=10**9, nbytes=2_000_000, trans=400_000,
    )
    above, below = neighbours(first, last, ROW)
    left, right = neighbours(*column_edges(mixed, above, below), COL)

    output, d_spatial, d_first, d_last, win, lnout, hidden, d_pre, d_branch, sums = call(
        sublayer_kernel,
        [
            ((PIX, C), BF16), ((PIX, C), F32), edge, edge, ((HB + 6, WCOL, C), BF16),
            ((PIX, C), BF16), ((PIX, HID), BF16), ((PIX, HID), BF16), ((PIX, C), BF16), ((8, HID), F32),
        ],
        mixed, above, below, left, right, cot, occ, dw_kernel, row(dw_bias), row(ln_gain),
        row(ln_bias), w_up, row(b_up), w_down, row(b_down), row(layer_scale),
        scratch=[pltpu.VMEM((HB + 6, WCOL, C), F32), pltpu.VMEM((PIX, C), F32)],
        flops=10**9, nbytes=4_000_000, trans=160_000,
    )

    d_above, d_below = neighbours(d_first, d_last, ROW)
    core = lax.axis_index("c").reshape(1)
    order = jnp.asarray(up_order(), BF16)
    record = ((N_X, REC, 128), BF16)
    mine, other = call(
        gradient_kernel, [record, record],
        core, order, lnout, hidden, d_pre, d_branch, win, d_spatial, sums,
        scratch=[
            pltpu.VMEM((HB + 6, WCOL, C), F32),
            pltpu.VMEM((TILES_L, HID, 128), F32),
            pltpu.VMEM((8 * SMALL, 128), F32),
        ],
        smem=(0,), flops=2 * 10**9, nbytes=4_000_000,
    )
    d_edges = column_edges(d_spatial.astype(BF16), d_above, d_below)
    d_left, d_right = neighbours(*d_edges, COL)

    got = lax.ppermute(other, "c", [(0, 1), (1, 0)])
    (part,) = call(core_sum_kernel, [record], mine, got, *d_edges, nbytes=3_000_000)
    part = lax.all_to_all(part, "x", 0, 0, tiled=True)
    (part,) = call(
        spread_kernel_after, [((N_YZ, 16 + SMALL, 128), BF16)], part, d_left, d_right,
        scratch=[pltpu.VMEM((REC, 128), F32)], nbytes=2_000_000,
    )
    part = lax.all_to_all(part, YZ, 0, 0, tiled=True)
    share, small = call(
        gather_kernel, [((16, 128), F32), ((N_X * N_C, SMALL, 128), F32)], part, nbytes=800_000
    )
    small = lax.all_to_all(small, CX, 0, 0, tiled=True)
    vectors = call(
        final_kernel, [((49, C), F32)] + [((1, C), F32)] * 5 + [((1, HID), F32)],
        small.reshape(-1, 128), nbytes=200_000,
    )
    share = share.reshape(2, 8 * 128)
    share = jnp.where(lax.axis_index("yh") == 0, share[:, :SHARE], share[:, 8 * 128 - SHARE :])
    (grad_mixed,) = call(
        spread_grad_kernel, [((PIX, C), F32)],
        d_spatial, d_above, d_below, d_left, d_right, cot, dw_kernel,
        scratch=[pltpu.VMEM((HB + 6, WCOL, C), F32)], flops=10**7, nbytes=1_000_000,
    )
    bias, gain, shift, b_down_grad, scale_grad, b_up_grad = [v.reshape(-1) for v in vectors[1:]]
    return (
        output.reshape(HB, WB, C), grad_mixed.reshape(HB, WB, C), share[0], share[1],
        vectors[0], bias, gain, shift, b_up_grad, b_down_grad, scale_grad,
    )


def spread_kernel_after(part, left, right, out, total):
    spread_kernel(part, out, total)


def solution(mesh):
    mesh = Mesh(mesh.devices.reshape(N_YL, N_X, N_C, N_Z, N_YH), ROW + COL)
    block = P(ROW, COL, None)
    in_specs = (block,) + (P(),) * 14 + (block, block)
    out_specs = (block, block, P(ROW + COL), P(ROW + COL)) + (P(),) * 7
    return jax.shard_map(body, mesh=mesh, in_specs=in_specs, out_specs=out_specs, check_vma=False)
```

```python
import numpy as np
import jax
import jax.numpy as jnp
from jax import lax
from jax.experimental import pallas as pl
from jax.experimental.pallas import tpu as pltpu
from jax.sharding import Mesh, PartitionSpec as P

ROW = ("yl", "x", "c")
COL = ("z", "yh")
YZ = ("yl", "z", "yh")
CX = ("c", "x")

F32 = jnp.float32
BF16 = jnp.bfloat16
EPS_NORM = 1e-06
GELU_SCALE = 0.7978845608028654
TS = 4
HB = 8
WB = 16
PIX = HB * WB
C = 384
HID = 1280
HEADS = 6
TILES_L = C // 128
N_YL, N_X, N_C, N_Z, N_YH = 4, 4, 2, 8, 2
N_ROW = N_YL * N_X * N_C
N_YZ = N_YL * N_Z * N_YH
SHARE = 960
SMALL = 24
REC = 1056
WCOL = 32
TILES = 8
HALO = 3
ROWS_M = HB + 4 * HALO
ROWS_D = HB + 2 * HALO
OWN = slice(HALO * WB, HALO * WB + PIX)

UP_TILES = (
    [(0, t) for t in range(8)],
    [(0, 7), (0, 8), (0, 9)] + [(1, t) for t in range(5)],
    [(1, t) for t in range(5, 10)] + [(2, t) for t in range(3)],
    [(2, t) for t in range(2, 10)],
)
DOWN_TILES = (
    [(0, t) for t in range(3)] + [(1, t) for t in range(3)] + [(2, 0), (2, 1)],
    [(2, 1), (2, 2)] + [(3, t) for t in range(3)] + [(4, t) for t in range(3)],
)


def call(kernel, outs, *args, scratch=(), smem=(), fence=(), flops=0, nbytes=0, trans=0, vmem=16):
    specs = [
        pl.BlockSpec(
            memory_space=pltpu.SMEM if i in smem else pl.ANY if i in fence else pltpu.VMEM
        )
        for i in range(len(args))
    ]
    return pl.pallas_call(
        kernel,
        out_shape=[jax.ShapeDtypeStruct(s, d) for s, d in outs],
        in_specs=specs,
        out_specs=[pl.BlockSpec(memory_space=pltpu.VMEM) for _ in outs],
        scratch_shapes=list(scratch),
        compiler_params=pltpu.CompilerParams(vmem_limit_bytes=vmem * 1024 * 1024),
        cost_estimate=pl.CostEstimate(flops=flops, bytes_accessed=nbytes, transcendentals=trans),
    )(*args)


def mm(a, b, dims=((1,), (0,))):
    return lax.dot_general(a, b, (dims, ((), ())), preferred_element_type=F32)


def head_scaled(values):
    block = lax.broadcasted_iota(jnp.int32, (C, C), 0) // 64
    same = (block == lax.broadcasted_iota(jnp.int32, (C, C), 1) // 64).astype(F32).astype(BF16)
    squares = values * values
    high = squares.astype(BF16)
    low = (squares - high.astype(F32)).astype(BF16)
    return values * lax.rsqrt(mm(high, same) + mm(low, same) + EPS_NORM)


def pool_kernel(feat, out):
    total = feat[0].astype(F32)
    for r in range(1, HB):
        total = total + feat[r].astype(F32)
    mean = (total * (1.0 / HB)).astype(BF16)
    for i in range(N_ROW):
        out[i] = mean


def prepare_kernel(tiles, after, feat, cot, layer_scale, d_branch, occ, first, last):
    pixel = lax.broadcasted_iota(jnp.int32, (PIX, 1), 0)
    tile = (pixel // (TS * WB)) * (WB // TS) + (pixel % WB) // TS
    weight = jnp.zeros((PIX, 1), F32)
    for i in range(TILES):
        weight = jnp.where(tile == tiles[i], 1.0, weight)
    occ[...] = weight
    value = (cot[...].astype(F32) * layer_scale[...] * weight).astype(BF16)
    d_branch[...] = value
    n = 2 * HALO * WB
    m = HALO * WB
    first[:n, :] = feat[:n, :]
    first[n:, :] = value[:m]
    last[:n, :] = feat[PIX - n :, :]
    last[n:, :] = value[PIX - m :]


def split_columns(rows):
    shaped = rows.reshape(rows.shape[0] // WB, 2, WB // 2, rows.shape[1])
    return [shaped[:, h].reshape(-1, rows.shape[1]) for h in range(2)]


def stacked_rows(feat, above, below):
    n = 2 * HALO * WB
    return jnp.concatenate([above[:n, :], feat[...], below[:n, :]], axis=0)


def query_kernel(feat, above, below, w_query, out):
    query = head_scaled(mm(stacked_rows(feat, above, below), w_query[...]))
    for h, half in enumerate(split_columns(query)):
        out[h] = half.astype(BF16)


def attention_kernel(
    scale, valid, pooled, query, feat, above, below, w_key, w_value, w_out,
    mixed, first, last, grid, edges,
):
    rows = pooled[...]
    all_keys = split_columns(head_scaled(mm(rows, w_key[...])))
    all_values = split_columns(mm(rows, w_value[...]))
    all_feat = split_columns(stacked_rows(feat, above, below).astype(F32))
    half = WB // 2
    n_query, n_keys = ROWS_M * half, N_ROW * half
    same = (
        lax.broadcasted_iota(jnp.int32, (n_query, n_keys), 0) % half
        == lax.broadcasted_iota(jnp.int32, (n_query, n_keys), 1) % half
    )
    lower = lax.broadcasted_iota(jnp.int32, (n_query, 128), 1) < 64
    row = lax.broadcasted_iota(jnp.int32, (n_query, 1), 0) // half
    inside = ((row >= 2 * HALO) | (valid[0] > 0)) & ((row < 2 * HALO + HB) | (valid[1] > 0))
    for h in range(2):
        keys, values = all_keys[h].astype(BF16), all_values[h].astype(BF16)
        pairs = []
        for pair in range(HEADS // 2):
            lanes = slice(128 * pair, 128 * pair + 128)
            q = query[h, :, lanes].astype(F32)
            parts = []
            for sub in range(2):
                q_half = jnp.where(lower if sub == 0 else ~lower, q, 0.0).astype(BF16)
                scores = mm(q_half, keys[:, lanes], ((1,), (1,)))
                weight = jnp.where(same, jnp.exp(scores * scale[2 * pair + sub]), 0.0)
                total = jnp.sum(weight, axis=1, keepdims=True)
                parts.append(mm(weight.astype(BF16), values[:, lanes]) / total)
            pairs.append(jnp.where(lower, parts[0], parts[1]).astype(BF16))
        attended = jnp.concatenate(pairs, axis=1)
        out = jnp.where(inside, all_feat[h] + mm(attended, w_out[...]), 0.0)
        grid[:, half * h : half * h + half, :] = out.reshape(ROWS_M, half, C)
    mixed[...] = grid[...].reshape(ROWS_M * WB, C).astype(BF16)
    column_edges(grid, edges, ROWS_M, first, last)


def column_edges(grid, edges, n_rows, first, last):
    edges[...] = jnp.zeros_like(edges)
    for r in range(n_rows):
        edges[0, HALO * r : HALO * r + HALO, :] = grid[r, :HALO, :]
        edges[1, HALO * r : HALO * r + HALO, :] = grid[r, WB - HALO :, :]
    first[...] = edges[0].astype(BF16)
    last[...] = edges[1].astype(BF16)


def fill_window(win, own, left, right, n_rows):
    for r in range(n_rows):
        win[r, 8 : 8 + WB, :] = own[r * WB : (r + 1) * WB, :].astype(F32)
    lcols = left[...].astype(F32)
    rcols = right[...].astype(F32)
    for r in range(n_rows):
        win[r, 8 - HALO : 8, :] = lcols[HALO * r : HALO * r + HALO]
        win[r, 8 + WB : 8 + WB + HALO, :] = rcols[HALO * r : HALO * r + HALO]


def depthwise(win, taps, n_out, start, flip, store):
    half = WB // 2
    for t in range(TILES_L):
        lanes = slice(128 * t, 128 * t + 128)
        for h in range(2):
            acc = [start(r, half * h, lanes) for r in range(n_out)]
            for dj in range(7):
                at = 8 - HALO + half * h + dj
                cols = [win[r, at : at + half, lanes] for r in range(n_out + 6)]
                for di in range(7):
                    tap = 7 * di + dj if not flip else 7 * (6 - di) + (6 - dj)
                    k = taps[tap : tap + 1, lanes]
                    for r in range(n_out):
                        acc[r] = acc[r] + cols[r + di] * k
            for r in range(n_out):
                store(r, half * h, lanes, acc[r])


def rowsum(a):
    return jnp.sum(a, axis=0, keepdims=True)


def sublayer_kernel(
    mixed, left, right, d_branch_own, above, below, cot, occ, taps, dw_bias, ln_gain, ln_bias,
    w_up, b_up, w_down, b_down, layer_scale,
    output, d_out, d_first, d_last, win_out, lnout_out, hidden_out, d_pre_out, sums,
    win, spat, grid, edges,
):
    fill_window(win, mixed, left, right, ROWS_M)
    win_out[...] = win[HALO : HALO + ROWS_D].astype(BF16)

    def start(r, j, lanes):
        return jnp.broadcast_to(dw_bias[:, lanes], (WB // 2, 128))

    def store(r, j, lanes, value):
        spat[r * WB + j : r * WB + j + WB // 2, lanes] = value

    depthwise(win, taps, ROWS_D, start, False, store)
    spatial = spat[...]
    center = spatial - jnp.mean(spatial, axis=1, keepdims=True)
    inv_std = lax.rsqrt(jnp.mean(center * center, axis=1, keepdims=True) + EPS_NORM)
    standard = center * inv_std
    gain = ln_gain[...]
    lnout = (standard * gain + ln_bias[...]).astype(BF16)
    lnout_out[...] = lnout[OWN]
    preact = mm(lnout, w_up[...]) + b_up[...]
    square = 0.044715 * preact * preact
    tanh_val = jnp.tanh(GELU_SCALE * preact * (1.0 + square))
    hidden = (0.5 * preact[OWN] * (1.0 + tanh_val[OWN])).astype(BF16)
    slope = 0.5 * (1.0 + tanh_val) + 0.5 * preact * (1.0 - tanh_val * tanh_val) * GELU_SCALE * (
        1.0 + 3.0 * square
    )
    hidden_out[...] = hidden
    n = 2 * HALO * WB
    d_branch_b = jnp.concatenate([above[n:, :], d_branch_own[...], below[n:, :]], axis=0)
    d_pre = mm(d_branch_b, w_down[...], ((1,), (1,))) * slope
    d_pre_b = d_pre.astype(BF16)
    d_pre_out[...] = d_pre_b[OWN]
    d_lnout = mm(d_pre_b, w_up[...], ((1,), (1,)))
    e = d_lnout * gain
    d_spatial = inv_std * (
        e
        - jnp.mean(e, axis=1, keepdims=True)
        - standard * jnp.mean(e * standard, axis=1, keepdims=True)
    )
    d_out[...] = d_spatial
    grid[...] = d_spatial.reshape(ROWS_D, WB, C)
    column_edges(grid, edges, ROWS_D, d_first, d_last)
    weight = occ[...]
    scale = layer_scale[...]
    cotan = cot[...].astype(F32)
    branch = (mm(hidden, w_down[...]) + b_down[...]) * weight
    output[...] = (mixed[2 * HALO * WB : 2 * HALO * WB + PIX, :].astype(F32) + scale * branch).astype(BF16)
    d_lnout = d_lnout[OWN]
    sums[0:1, :C] = rowsum(d_spatial[OWN])
    sums[1:2, :C] = rowsum(d_lnout * standard[OWN])
    sums[2:3, :C] = rowsum(d_lnout)
    sums[3:4, :C] = rowsum(cotan * scale * weight)
    sums[4:5, :C] = rowsum(cotan * branch)
    sums[5:6, :] = rowsum(d_pre[OWN])


def up_order():
    chan = np.arange(C).reshape(N_YL, N_X, N_C, N_Z // 2, 3).transpose(4, 2, 1, 0, 3).reshape(-1)
    return (np.arange(C)[:, None] == chan[None, :]).astype(np.float32)


def gradient_kernel(
    core, order, lnout, hidden, d_pre, d_branch, win_in, d_spatial, sums, mine, other, win, down, small
):
    is_zero = core[0] == 0

    def put(row, x, zero, one):
        size = zero.shape[0]
        mine[x, row : row + size, :] = jnp.where(is_zero, zero, one).astype(BF16)
        other[x, row : row + size, :] = jnp.where(is_zero, one, zero).astype(BF16)

    ordered = mm(lnout[...], order[...]).astype(BF16)
    ups = [mm(ordered[:, 128 * r : 128 * r + 128], d_pre[...], ((0,), (0,))) for r in range(3)]
    for q in range(4):
        for k, (r, t) in enumerate(UP_TILES[q]):
            for x in range(N_X):
                pair = [ups[r][64 * c + 16 * x : 64 * c + 16 * x + 16, 128 * t : 128 * t + 128] for c in range(2)]
                put((q * 8 + k) * 16, x, *pair)
    full = mm(hidden[...], d_branch[...], ((0,), (0,)))
    for t in range(TILES_L):
        down[t] = full[:, 128 * t : 128 * t + 128]
    for yh in range(2):
        for k, (s, t) in enumerate(DOWN_TILES[yh]):
            for x in range(N_X):
                for two in range(2):
                    pair = [
                        jnp.concatenate(
                            [
                                down[t, pl.ds(5 * (64 * yl + 16 * x + 8 * c) + s, 8, stride=5), :]
                                for yl in (2 * two, 2 * two + 1)
                            ],
                            axis=0,
                        )
                        for c in range(2)
                    ]
                    put(512 + (yh * 8 + k) * 32 + 16 * two, x, *pair)
    win[...] = win_in[...].astype(F32)
    small[...] = jnp.zeros_like(small)
    for t in range(TILES_L):
        lanes = slice(128 * t, 128 * t + 128)
        d_rows = [d_spatial[(HALO + r) * WB : (HALO + r + 1) * WB, lanes] for r in range(HB)]
        for dj in range(7):
            cols = [win[r, 5 + dj : 5 + dj + WB, lanes] for r in range(HB + 6)]
            for di in range(7):
                acc = cols[di] * d_rows[0]
                for r in range(1, HB):
                    acc = acc + cols[r + di] * d_rows[r]
                at = 56 * t + 7 * di + dj
                small[at : at + 1, :] = rowsum(acc)
    for i in range(5):
        for t in range(TILES_L):
            small[161 + 3 * i + t : 162 + 3 * i + t, :] = sums[i : i + 1, 128 * t : 128 * t + 128]
    for t in range(HID // 128):
        small[176 + t : 177 + t, :] = sums[5:6, 128 * t : 128 * t + 128]
    for x in range(N_X):
        pair = [
            jnp.concatenate([small[96 * c + 24 * x : 96 * c + 24 * x + 24], jnp.zeros((8, 128), F32)], axis=0)
            for c in range(2)
        ]
        put(1024, x, *pair)


def spread_kernel(part, d_first, d_last, out, d_first_out, d_last_out, total):
    d_first_out[...] = d_first[...]
    d_last_out[...] = d_last[...]
    total[...] = (
        (part[0].astype(F32) + part[1].astype(F32)) + (part[2].astype(F32) + part[3].astype(F32))
    )
    small = total[1024 : 1024 + SMALL, :]
    for yl in range(N_YL):
        for z in range(N_Z):
            for yh in range(N_YH):
                q = (z % 2) * 2 + yh
                up = total[pl.ds(q * 128 + yl * 4 + z // 2, 8, stride=16), :]
                down = total[pl.ds(512 + yh * 256 + yl * 8 + z, 8, stride=32), :]
                record = jnp.concatenate([up, down, small], axis=0)
                out[(yl * N_Z + z) * N_YH + yh] = record.astype(BF16)


def gather_kernel(part, share, small):
    total = part[0].astype(F32)
    for i in range(1, N_YZ):
        total = total + part[i].astype(F32)
    share[...] = total[:16]
    for i in range(N_X * N_C):
        small[i] = total[16:]


def final_kernel(small, dw, *vectors):
    for t in range(TILES_L):
        dw[:, 128 * t : 128 * t + 128] = small[56 * t : 56 * t + 49, :]
    for i in range(5):
        for t in range(TILES_L):
            vectors[i][pl.ds(128 * t, 128)] = small[161 + 3 * i + t, :]
    for t in range(HID // 128):
        vectors[5][pl.ds(128 * t, 128)] = small[176 + t, :]


def grad_mixed_kernel(d_all, left, right, cot, taps, out, win):
    fill_window(win, d_all, left, right, ROWS_D)

    def start(r, j, lanes):
        return cot[r * WB : (r + 1) * WB, lanes].astype(F32)[j : j + WB // 2]

    def store(r, j, lanes, value):
        out[r * WB + j : r * WB + j + WB // 2, lanes] = value

    depthwise(win, taps, HB, start, True, store)


def core_sum_kernel(mine, got, out):
    out[...] = (mine[...].astype(F32) + got[...].astype(F32)).astype(BF16)


def neighbours(before_edge, after_edge, axes):
    size = lax.axis_size(axes)
    up = [(i, i + 1) for i in range(size - 1)]
    down = [(i + 1, i) for i in range(size - 1)]
    return lax.ppermute(after_edge, axes, up), lax.ppermute(before_edge, axes, down)


def body(
    features, w_query, w_key, w_value, w_out, logit_scale, dw_kernel, dw_bias, ln_gain, ln_bias,
    w_up, b_up, w_down, b_down, layer_scale, cotangent, tile_list,
):
    row = lambda v: v.reshape(1, -1)
    flat = features.reshape(PIX, C)
    cot = cotangent.reshape(PIX, C)

    (copies,) = call(pool_kernel, [((N_ROW, WB, C), BF16)], features, nbytes=500_000)
    pooled = lax.all_to_all(copies, ROW, 0, 0, tiled=True).reshape(N_ROW * WB, C)

    shared = ((3 * HALO * WB, C), BF16)
    d_branch, occ, feat_first, feat_last = call(
        prepare_kernel, [((PIX, C), BF16), ((PIX, 1), F32), shared, shared],
        tile_list.reshape(-1), copies, flat, cot, row(layer_scale), smem=(0,), fence=(1,), nbytes=800_000,
    )
    above, below = neighbours(feat_first, feat_last, ROW)
    (query,) = call(
        query_kernel, [((2, ROWS_M * WB // 2, C), BF16)], flat, above, below, w_query,
        flops=2 * 10**8, nbytes=900_000,
    )
    at_row = lax.axis_index(ROW)
    valid = jnp.stack([at_row > 0, at_row < N_ROW - 1]).astype(jnp.int32)
    edge = ((64, C), BF16)
    mixed, first, last = call(
        attention_kernel, [((ROWS_M * WB, C), BF16), edge, edge],
        logit_scale, valid, pooled, query, flat, above, below, w_key, w_value, w_out,
        scratch=[pltpu.VMEM((ROWS_M, WB, C), F32), pltpu.VMEM((2, 64, C), F32)],
        smem=(0, 1), flops=10**9, nbytes=2_000_000, trans=500_000,
    )
    left, right = neighbours(first, last, COL)

    d_edge = ((48, C), BF16)
    output, d_all, d_first, d_last, win, lnout, hidden, d_pre, sums = call(
        sublayer_kernel,
        [
            ((PIX, C), BF16), ((ROWS_D * WB, C), F32), d_edge, d_edge, ((ROWS_D, WCOL, C), BF16),
            ((PIX, C), BF16), ((PIX, HID), BF16), ((PIX, HID), BF16), ((8, HID), F32),
        ],
        mixed, left, right, d_branch, above, below, cot, occ, dw_kernel, row(dw_bias),
        row(ln_gain), row(ln_bias), w_up, row(b_up), w_down, row(b_down), row(layer_scale),
        scratch=[
            pltpu.VMEM((ROWS_M, WCOL, C), F32), pltpu.VMEM((ROWS_D * WB, C), F32),
            pltpu.VMEM((ROWS_D, WB, C), F32), pltpu.VMEM((2, 48, C), F32),
        ],
        flops=10**9, nbytes=4_000_000, trans=300_000, vmem=24,
    )

    core = lax.axis_index("c").reshape(1)
    order = jnp.asarray(up_order(), BF16)
    record = ((N_X, REC, 128), BF16)
    mine, other = call(
        gradient_kernel, [record, record],
        core, order, lnout, hidden, d_pre, d_branch, win, d_all, sums,
        scratch=[
            pltpu.VMEM((ROWS_D, WCOL, C), F32),
            pltpu.VMEM((TILES_L, HID, 128), F32),
            pltpu.VMEM((8 * SMALL, 128), F32),
        ],
        smem=(0,), flops=2 * 10**9, nbytes=4_000_000,
    )
    got = lax.ppermute(other, "c", [(0, 1), (1, 0)])
    (part,) = call(core_sum_kernel, [record], mine, got, nbytes=3_000_000)
    part = lax.all_to_all(part, "x", 0, 0, tiled=True)
    part, d_first, d_last = call(
        spread_kernel, [((N_YZ, 16 + SMALL, 128), BF16), d_edge, d_edge], part, d_first, d_last,
        scratch=[pltpu.VMEM((REC, 128), F32)], nbytes=2_000_000,
    )
    part = lax.all_to_all(part, YZ, 0, 0, tiled=True)
    d_left, d_right = neighbours(d_first, d_last, COL)
    share, small = call(
        gather_kernel, [((16, 128), F32), ((N_X * N_C, SMALL, 128), F32)], part, nbytes=800_000
    )
    small = lax.all_to_all(small, CX, 0, 0, tiled=True)
    vectors = call(
        final_kernel, [((49, C), F32)] + [((C,), F32)] * 5 + [((HID,), F32)],
        small.reshape(-1, 128), nbytes=200_000,
    )
    share = share.reshape(2, 8 * 128)
    share = jnp.where(lax.axis_index("yh") == 0, share[:, :SHARE], share[:, 8 * 128 - SHARE :])
    (grad_mixed,) = call(
        grad_mixed_kernel, [((PIX, C), F32)], d_all, d_left, d_right, cot, dw_kernel,
        scratch=[pltpu.VMEM((ROWS_D, WCOL, C), F32)], flops=10**7, nbytes=1_000_000,
    )
    bias, gain, shift, b_down_grad, scale_grad, b_up_grad = vectors[1:]
    return (
        output.reshape(HB, WB, C), grad_mixed.reshape(HB, WB, C), share[0], share[1],
        vectors[0], bias, gain, shift, b_up_grad, b_down_grad, scale_grad,
    )


def solution(mesh):
    mesh = Mesh(mesh.devices.reshape(N_YL, N_X, N_C, N_Z, N_YH), ROW + COL)
    block = P(ROW, COL, None)
    in_specs = (block,) + (P(),) * 14 + (block, block)
    out_specs = (block, block, P(ROW + COL), P(ROW + COL)) + (P(),) * 7
    return jax.shard_map(body, mesh=mesh, in_specs=in_specs, out_specs=out_specs, check_vma=False)
```

```python
import numpy as np
import jax
import jax.numpy as jnp
from jax import lax
from jax.experimental import pallas as pl
from jax.experimental.pallas import tpu as pltpu
from jax.sharding import Mesh, PartitionSpec as P

ROW = ("yl", "x", "c")
COL = ("z", "yh")
YZ = ("yl", "z", "yh")
CX = ("c", "x")

F32 = jnp.float32
BF16 = jnp.bfloat16
EPS_NORM = 1e-06
GELU_SCALE = 0.7978845608028654
TS = 4
HB = 8
WB = 16
PIX = HB * WB
C = 384
HID = 1280
HEADS = 6
TILES_L = C // 128
N_YL, N_X, N_C, N_Z, N_YH = 4, 4, 2, 8, 2
N_ROW = N_YL * N_X * N_C
N_YZ = N_YL * N_Z * N_YH
SHARE = 960
SMALL = 24
REC = 1056
WCOL = 32
TILES = 8
HALO = 3
ROWS_M = HB + 4 * HALO
ROWS_D = HB + 2 * HALO
RIGHT_COT = 2 * HALO * ROWS_M
RIGHT_HIT = RIGHT_COT + HALO * ROWS_D
RIGHT = 176
LEFT_OUT = 2 * HALO * ROWS_D
LEFT = 112
HALF = WB // 2
PIX_H = HB * HALF
OWN = slice(HALO * HALF, HALO * HALF + PIX_H)

UP_TILES = (
    [(0, t) for t in range(8)],
    [(0, 7), (0, 8), (0, 9)] + [(1, t) for t in range(5)],
    [(1, t) for t in range(5, 10)] + [(2, t) for t in range(3)],
    [(2, t) for t in range(2, 10)],
)
DOWN_TILES = (
    [(0, t) for t in range(3)] + [(1, t) for t in range(3)] + [(2, 0), (2, 1)],
    [(2, 1), (2, 2)] + [(3, t) for t in range(3)] + [(4, t) for t in range(3)],
)


def call(kernel, outs, *args, scratch=(), smem=(), fence=(), flops=0, nbytes=0, trans=0, vmem=16):
    specs = [
        pl.BlockSpec(
            memory_space=pltpu.SMEM if i in smem else pl.ANY if i in fence else pltpu.VMEM
        )
        for i in range(len(args))
    ]
    return pl.pallas_call(
        kernel,
        out_shape=[jax.ShapeDtypeStruct(s, d) for s, d in outs],
        in_specs=specs,
        out_specs=[pl.BlockSpec(memory_space=pltpu.VMEM) for _ in outs],
        scratch_shapes=list(scratch),
        compiler_params=pltpu.CompilerParams(vmem_limit_bytes=vmem * 1024 * 1024),
        cost_estimate=pl.CostEstimate(flops=flops, bytes_accessed=nbytes, transcendentals=trans),
    )(*args)


def mm(a, b, dims=((1,), (0,))):
    return lax.dot_general(a, b, (dims, ((), ())), preferred_element_type=F32)


def head_scaled(values):
    block = lax.broadcasted_iota(jnp.int32, (C, C), 0) // 64
    same = (block == lax.broadcasted_iota(jnp.int32, (C, C), 1) // 64).astype(F32).astype(BF16)
    squares = values * values
    high = squares.astype(BF16)
    low = (squares - high.astype(F32)).astype(BF16)
    return values * lax.rsqrt(mm(high, same) + mm(low, same) + EPS_NORM)


def pool_kernel(feat, out):
    total = feat[0].astype(F32)
    for r in range(1, HB):
        total = total + feat[r].astype(F32)
    mean = (total * (1.0 / HB)).astype(BF16)
    for i in range(N_ROW):
        out[i] = mean


def prepare_kernel(tiles, after, feat, cot, masked, first, last):
    pixel = lax.broadcasted_iota(jnp.int32, (PIX, 1), 0)
    value = (cot[...].astype(F32) * occupied(tiles, pixel // WB, pixel % WB)).astype(BF16)
    masked[...] = value
    n = 2 * HALO * WB
    m = HALO * WB
    first[:n, :] = feat[:n, :]
    first[n:, :] = value[:m]
    last[:n, :] = feat[PIX - n :, :]
    last[n:, :] = value[PIX - m :]


def occupied(tiles, row, col):
    tile = (row // TS) * (WB // TS) + col // TS
    weight = jnp.zeros(tile.shape, F32)
    for i in range(TILES):
        weight = jnp.where(tile == tiles[i], 1.0, weight)
    return weight


def split_columns(rows):
    shaped = rows.reshape(rows.shape[0] // WB, 2, WB // 2, rows.shape[1])
    return [shaped[:, h].reshape(-1, rows.shape[1]) for h in range(2)]


def stacked_rows(feat, above, below):
    n = 2 * HALO * WB
    return jnp.concatenate([above[:n, :], feat[...], below[:n, :]], axis=0)


def query_kernel(feat, above, below, w_query, out):
    query = head_scaled(mm(stacked_rows(feat, above, below), w_query[...]))
    for h, half in enumerate(split_columns(query)):
        out[h] = half.astype(BF16)


def attention_kernel(
    scale, valid, tiles, pooled, query, feat, masked, above, below, w_key, w_value, w_out,
    mixed, send, grid, cot_grid, edges,
):
    rows = pooled[...]
    all_keys = split_columns(head_scaled(mm(rows, w_key[...])))
    all_values = split_columns(mm(rows, w_value[...]))
    all_feat = split_columns(stacked_rows(feat, above, below).astype(F32))
    half = WB // 2
    n_query, n_keys = ROWS_M * half, N_ROW * half
    same = (
        lax.broadcasted_iota(jnp.int32, (n_query, n_keys), 0) % half
        == lax.broadcasted_iota(jnp.int32, (n_query, n_keys), 1) % half
    )
    lower = lax.broadcasted_iota(jnp.int32, (n_query, 128), 1) < 64
    row = lax.broadcasted_iota(jnp.int32, (n_query, 1), 0) // half
    inside = ((row >= 2 * HALO) | (valid[0] > 0)) & ((row < 2 * HALO + HB) | (valid[1] > 0))
    for h in range(2):
        keys, values = all_keys[h].astype(BF16), all_values[h].astype(BF16)
        pairs = []
        for pair in range(HEADS // 2):
            lanes = slice(128 * pair, 128 * pair + 128)
            q = query[h, :, lanes].astype(F32)
            parts = []
            for sub in range(2):
                q_half = jnp.where(lower if sub == 0 else ~lower, q, 0.0).astype(BF16)
                scores = mm(q_half, keys[:, lanes], ((1,), (1,)))
                weight = jnp.where(same, jnp.exp(scores * scale[2 * pair + sub]), 0.0)
                total = jnp.sum(weight, axis=1, keepdims=True)
                parts.append(mm(weight.astype(BF16), values[:, lanes]) / total)
            pairs.append(jnp.where(lower, parts[0], parts[1]).astype(BF16))
        attended = jnp.concatenate(pairs, axis=1)
        out = jnp.where(inside, all_feat[h] + mm(attended, w_out[...]), 0.0)
        grid[:, half * h : half * h + half, :] = out.reshape(ROWS_M, half, C)
    mixed[...] = grid[...].reshape(ROWS_M * WB, C).astype(BF16)
    cot_grid[...] = cot_rows(masked, above, below).astype(F32).reshape(ROWS_D, WB, C)
    edges[...] = jnp.zeros_like(edges)
    for r in range(ROWS_M):
        edges[6 * r : 6 * r + 6, :] = grid[r, WB - 6 :, :]
    for r in range(ROWS_D):
        at = RIGHT_COT + HALO * r
        edges[at : at + HALO, :] = cot_grid[r, WB - HALO :, :]
    tile_row = lax.broadcasted_iota(jnp.int32, (1, C), 1) // 128 * TS
    edges[RIGHT_HIT : RIGHT_HIT + 1, :] = occupied(tiles, tile_row, jnp.full((1, C), WB - 1))
    send[...] = edges[...].astype(BF16)


def cot_rows(masked, above, below):
    n = 2 * HALO * WB
    return jnp.concatenate([above[n:, :], masked[...], below[n:, :]], axis=0)


def border_mask(is_first, dj, start, size):
    u = lax.broadcasted_iota(jnp.int32, (size, 128), 0) + start
    crosses = (u < HALO) != (u + dj < 2 * HALO)
    return jnp.where(crosses & is_first, 0.0, 1.0)


def depthwise(win, taps, n_out, base, halves, start, flip, store, is_first=None):
    masks = [None] * 7
    if is_first is not None:
        masks = [border_mask(is_first, dj, 0, HALF) for dj in range(7)]
    for t in range(TILES_L):
        lanes = slice(128 * t, 128 * t + 128)
        for h in halves:
            acc = [start(r, h, lanes) for r in range(n_out)]
            for dj in range(7):
                at = base + HALF * h + dj
                cols = [win[r, at : at + HALF, lanes] for r in range(n_out + 6)]
                if h == 0 and dj != 3 and is_first is not None:
                    cols = [col * masks[dj] for col in cols]
                for di in range(7):
                    tap = 7 * di + dj if not flip else 7 * (6 - di) + (6 - dj)
                    k = taps[tap : tap + 1, lanes]
                    for r in range(n_out):
                        acc[r] = acc[r] + cols[r + di] * k
            for r in range(n_out):
                store(r, h, lanes, acc[r])


def rowsum(a):
    return jnp.sum(a, axis=0, keepdims=True)


def right_half_kernel(tiles, mixed, masked, above, below, *refs):
    sublayer(1, None, tiles, mixed, None, masked, above, below, *refs)


def left_half_kernel(at_first, tiles, mixed, got, masked, above, below, *refs):
    sublayer(0, at_first, tiles, mixed, got, masked, above, below, *refs)


def sublayer(
    h, at_first, tiles, mixed, got, masked, above, below, taps, dw_bias, ln_gain, ln_bias,
    w_up, b_up, w_down, b_down, layer_scale, output, d_out, lnout_out, hidden_out, d_pre_out,
    d_branch_out, sums, *refs,
):
    if h == 0:
        win_out, send, win, grid, spat, edges = refs
        is_first = at_first[0] > 0
        halo = got[...].astype(F32)
    else:
        win, grid, spat = refs
        is_first = None
    for r in range(ROWS_M):
        win[r, 8 : 8 + WB, :] = mixed[r * WB : (r + 1) * WB, :].astype(F32)
        if h == 0:
            win[r, 2:8, :] = halo[6 * r : 6 * r + 6]
    grid[:, 8 : 8 + WB, :] = cot_rows(masked, above, below).astype(F32).reshape(ROWS_D, WB, C)
    pixel = lax.broadcasted_iota(jnp.int32, (PIX_H, 1), 0)
    row, col = pixel // HALF, pixel % HALF + HALF * h - HALO
    weight = occupied(tiles, row, jnp.maximum(col, 0))
    if h == 0:
        win_out[...] = win[HALO : HALO + ROWS_D].astype(BF16)
        for r in range(ROWS_D):
            at = RIGHT_COT + HALO * r
            grid[r, 8 - HALO : 8, :] = halo[at : at + HALO]
        hits = halo[RIGHT_HIT : RIGHT_HIT + 1]
        before = jnp.where(row < TS, hits[:, 0:1], hits[:, 128:129])
        weight = jnp.where(col < 0, before, weight)
    here = slice(8 - HALO + HALF * h, 8 - HALO + HALF * h + HALF)
    cotan = grid[:, here, :].reshape(ROWS_D * HALF, C)

    def start(r, h, lanes):
        return jnp.broadcast_to(dw_bias[:, lanes], (HALF, 128))

    def store(r, h, lanes, value):
        spat[r * HALF : (r + 1) * HALF, lanes] = value

    depthwise(win, taps, ROWS_D, 2, (h,), start, False, store, is_first)
    spatial = spat[...]
    center = spatial - jnp.mean(spatial, axis=1, keepdims=True)
    inv_std = lax.rsqrt(jnp.mean(center * center, axis=1, keepdims=True) + EPS_NORM)
    standard = center * inv_std
    gain = ln_gain[...]
    lnout = (standard * gain + ln_bias[...]).astype(BF16)
    lnout_out[...] = lnout[OWN]
    preact = mm(lnout, w_up[...]) + b_up[...]
    square = 0.044715 * preact * preact
    tanh_val = jnp.tanh(GELU_SCALE * preact * (1.0 + square))
    hidden = (0.5 * preact[OWN] * (1.0 + tanh_val[OWN])).astype(BF16)
    slope = 0.5 * (1.0 + tanh_val) + 0.5 * preact * (1.0 - tanh_val * tanh_val) * GELU_SCALE * (
        1.0 + 3.0 * square
    )
    hidden_out[...] = hidden
    scale = layer_scale[...]
    d_branch = cotan * scale
    d_branch_b = d_branch.astype(BF16)
    d_branch_out[...] = d_branch_b[OWN]
    d_pre = mm(d_branch_b, w_down[...], ((1,), (1,))) * slope
    d_pre_b = d_pre.astype(BF16)
    d_pre_out[...] = d_pre_b[OWN]
    d_lnout = mm(d_pre_b, w_up[...], ((1,), (1,)))
    e = d_lnout * gain
    d_spatial = inv_std * (
        e
        - jnp.mean(e, axis=1, keepdims=True)
        - standard * jnp.mean(e * standard, axis=1, keepdims=True)
    )
    d_out[...] = d_spatial
    branch = (mm(hidden, w_down[...]) + b_down[...]) * weight
    base = win[2 * HALO : 2 * HALO + HB, here, :].reshape(PIX_H, C)
    out = base + scale * branch
    output[...] = out.astype(BF16)
    if h == 0:
        edges[...] = jnp.zeros_like(edges)
        for r in range(ROWS_D):
            edges[6 * r : 6 * r + 6, :] = d_spatial[r * HALF : r * HALF + 6]
        for r in range(HB):
            at = LEFT_OUT + HALO * r
            edges[at : at + HALO, :] = out[r * HALF : r * HALF + HALO]
        send[...] = edges[...].astype(BF16)
    d_lnout = d_lnout[OWN]
    sums[0:1, :C] = rowsum(d_spatial[OWN])
    sums[1:2, :C] = rowsum(d_lnout * standard[OWN])
    sums[2:3, :C] = rowsum(d_lnout)
    sums[3:4, :C] = rowsum(d_branch[OWN])
    sums[4:5, :C] = rowsum(cotan[OWN] * branch)
    sums[5:6, :] = rowsum(d_pre[OWN])


def up_order():
    chan = np.arange(C).reshape(N_YL, N_X, N_C, N_Z // 2, 3).transpose(4, 2, 1, 0, 3).reshape(-1)
    return (np.arange(C)[:, None] == chan[None, :]).astype(np.float32)


def gradient_kernel(
    flags, order, win_in, *refs
):
    halves = [refs[:6], refs[6:12]]
    mine, other, win, down, small = refs[12:]
    lnout, hidden, d_pre, d_branch = [
        jnp.concatenate([halves[0][i][...], halves[1][i][...]], axis=0) for i in range(4)
    ]
    is_zero = flags[0] == 0
    is_first = flags[1] > 0

    def put(row, x, zero, one):
        size = zero.shape[0]
        mine[x, row : row + size, :] = jnp.where(is_zero, zero, one).astype(BF16)
        other[x, row : row + size, :] = jnp.where(is_zero, one, zero).astype(BF16)

    ordered = mm(lnout, order[...]).astype(BF16)
    ups = [mm(ordered[:, 128 * r : 128 * r + 128], d_pre, ((0,), (0,))) for r in range(3)]
    for q in range(4):
        for k, (r, t) in enumerate(UP_TILES[q]):
            for x in range(N_X):
                pair = [ups[r][64 * c + 16 * x : 64 * c + 16 * x + 16, 128 * t : 128 * t + 128] for c in range(2)]
                put((q * 8 + k) * 16, x, *pair)
    full = mm(hidden, d_branch, ((0,), (0,)))
    for t in range(TILES_L):
        down[t] = full[:, 128 * t : 128 * t + 128]
    for yh in range(2):
        for k, (s, t) in enumerate(DOWN_TILES[yh]):
            for x in range(N_X):
                for two in range(2):
                    pair = [
                        jnp.concatenate(
                            [
                                down[t, pl.ds(5 * (64 * yl + 16 * x + 8 * c) + s, 8, stride=5), :]
                                for yl in (2 * two, 2 * two + 1)
                            ],
                            axis=0,
                        )
                        for c in range(2)
                    ]
                    put(512 + (yh * 8 + k) * 32 + 16 * two, x, *pair)
    win[...] = win_in[...].astype(F32)
    small[...] = jnp.zeros_like(small)
    masks = [border_mask(is_first, dj, 0, HALF) for dj in range(7)]
    for t in range(TILES_L):
        lanes = slice(128 * t, 128 * t + 128)
        d_rows = [
            [d[(HALO + r) * HALF : (HALO + r + 1) * HALF, lanes] for r in range(HB)]
            for d in (halves[0][4], halves[1][4])
        ]
        for dj in range(7):
            cols = [
                [win[r, 2 + dj + HALF * h : 2 + dj + HALF * h + HALF, lanes] for r in range(HB + 6)]
                for h in range(2)
            ]
            if dj != 3:
                cols[0] = [col * masks[dj] for col in cols[0]]
            for di in range(7):
                acc = cols[0][di] * d_rows[0][0]
                for h in range(2):
                    for r in range(1 - h, HB):
                        acc = acc + cols[h][r + di] * d_rows[h][r]
                at = 56 * t + 7 * di + dj
                small[at : at + 1, :] = rowsum(acc)
    sums = halves[0][5][...] + halves[1][5][...]
    for i in range(5):
        for t in range(TILES_L):
            small[161 + 3 * i + t : 162 + 3 * i + t, :] = sums[i : i + 1, 128 * t : 128 * t + 128]
    for t in range(HID // 128):
        small[176 + t : 177 + t, :] = sums[5:6, 128 * t : 128 * t + 128]
    for x in range(N_X):
        pair = [
            jnp.concatenate([small[96 * c + 24 * x : 96 * c + 24 * x + 24], jnp.zeros((8, 128), F32)], axis=0)
            for c in range(2)
        ]
        put(1024, x, *pair)


def spread_kernel(part, send, out, send_out, total):
    send_out[...] = send[...]
    total[...] = (
        (part[0].astype(F32) + part[1].astype(F32)) + (part[2].astype(F32) + part[3].astype(F32))
    )
    small = total[1024 : 1024 + SMALL, :]
    for yl in range(N_YL):
        for z in range(N_Z):
            for yh in range(N_YH):
                q = (z % 2) * 2 + yh
                up = total[pl.ds(q * 128 + yl * 4 + z // 2, 8, stride=16), :]
                down = total[pl.ds(512 + yh * 256 + yl * 8 + z, 8, stride=32), :]
                record = jnp.concatenate([up, down, small], axis=0)
                out[(yl * N_Z + z) * N_YH + yh] = record.astype(BF16)


def gather_kernel(part, share, small):
    total = part[0].astype(F32)
    for i in range(1, N_YZ):
        total = total + part[i].astype(F32)
    share[...] = total[:16]
    for i in range(N_X * N_C):
        small[i] = total[16:]


def final_kernel(small, dw, *vectors):
    for t in range(TILES_L):
        dw[:, 128 * t : 128 * t + 128] = small[56 * t : 56 * t + 49, :]
    for i in range(5):
        for t in range(TILES_L):
            vectors[i][pl.ds(128 * t, 128)] = small[161 + 3 * i + t, :]
    for t in range(HID // 128):
        vectors[5][pl.ds(128 * t, 128)] = small[176 + t, :]


def finish_kernel(
    at_ends, after, d_left, d_right, out_left, out_right, got, cot, taps, grad, output, win
):
    halo = got[...].astype(F32)
    column = lax.broadcasted_iota(jnp.int32, (HALF, 1), 0)
    here = jnp.where((column < HALO) & (at_ends[0] > 0), 0.0, 1.0)
    beyond = lax.broadcasted_iota(jnp.int32, (6, 1), 0)
    there = jnp.where((beyond >= HALO) & (at_ends[1] > 0), 0.0, 1.0)
    for r in range(HB):
        at = LEFT_OUT + HALO * r
        win[r, 8 : 8 + HALF, :] = out_left[r * HALF : (r + 1) * HALF, :].astype(F32)
        win[r, 8 + HALF : 8 + WB, :] = out_right[r * HALF : (r + 1) * HALF, :].astype(F32)
        win[r, 8 + WB : 8 + WB + HALO, :] = halo[at : at + HALO]
    output[...] = win[:HB, 8 + HALO : 8 + HALO + WB, :].reshape(PIX, C).astype(BF16)
    for r in range(ROWS_D):
        win[r, 8 : 8 + HALF, :] = d_left[r * HALF : (r + 1) * HALF, :] * here
        win[r, 8 + HALF : 8 + WB, :] = d_right[r * HALF : (r + 1) * HALF, :]
        win[r, 8 + WB : 14 + WB, :] = halo[6 * r : 6 * r + 6] * there

    def start(r, h, lanes):
        return cot[r * WB : (r + 1) * WB, lanes].astype(F32)[HALF * h : HALF * h + HALF]

    def store(r, h, lanes, value):
        at = r * WB + HALF * h
        grad[at : at + HALF, lanes] = value

    depthwise(win, taps, HB, 8, (0, 1), start, True, store)


def core_sum_kernel(mine, got, out):
    out[...] = (mine[...].astype(F32) + got[...].astype(F32)).astype(BF16)


def neighbours(before_edge, after_edge, axes):
    size = lax.axis_size(axes)
    up = [(i, i + 1) for i in range(size - 1)]
    down = [(i + 1, i) for i in range(size - 1)]
    return lax.ppermute(after_edge, axes, up), lax.ppermute(before_edge, axes, down)


def body(
    features, w_query, w_key, w_value, w_out, logit_scale, dw_kernel, dw_bias, ln_gain, ln_bias,
    w_up, b_up, w_down, b_down, layer_scale, cotangent, tile_list,
):
    row = lambda v: v.reshape(1, -1)
    flat = features.reshape(PIX, C)
    cot = cotangent.reshape(PIX, C)

    (copies,) = call(pool_kernel, [((N_ROW, WB, C), BF16)], features, nbytes=500_000)
    pooled = lax.all_to_all(copies, ROW, 0, 0, tiled=True).reshape(N_ROW * WB, C)

    shared = ((3 * HALO * WB, C), BF16)
    tiles = tile_list.reshape(-1)
    masked, feat_first, feat_last = call(
        prepare_kernel, [((PIX, C), BF16), shared, shared],
        tiles, copies, flat, cot, smem=(0,), fence=(1,), nbytes=800_000,
    )
    above, below = neighbours(feat_first, feat_last, ROW)
    (query,) = call(
        query_kernel, [((2, ROWS_M * WB // 2, C), BF16)], flat, above, below, w_query,
        flops=2 * 10**8, nbytes=900_000,
    )
    at_row = lax.axis_index(ROW)
    valid = jnp.stack([at_row > 0, at_row < N_ROW - 1]).astype(jnp.int32)
    mixed, send = call(
        attention_kernel, [((ROWS_M * WB, C), BF16), ((RIGHT, C), BF16)],
        logit_scale, valid, tiles, pooled, query, flat, masked, above, below, w_key, w_value, w_out,
        scratch=[
            pltpu.VMEM((ROWS_M, WB, C), F32), pltpu.VMEM((ROWS_D, WB, C), F32),
            pltpu.VMEM((RIGHT, C), F32),
        ],
        smem=(0, 1, 2), flops=10**9, nbytes=2_000_000, trans=500_000,
    )
    n_col = lax.axis_size(COL)
    at_col = lax.axis_index(COL)
    got = lax.ppermute(send, COL, [(i, (i + 1) % n_col) for i in range(n_col)])
    ends = jnp.stack([at_col == 0, at_col == n_col - 1]).astype(jnp.int32)

    half_outs = [
        ((PIX_H, C), BF16), ((ROWS_D * HALF, C), F32), ((PIX_H, C), BF16), ((PIX_H, HID), BF16),
        ((PIX_H, HID), BF16), ((PIX_H, C), BF16), ((8, HID), F32),
    ]
    half_scratch = [
        pltpu.VMEM((ROWS_M, WCOL, C), F32), pltpu.VMEM((ROWS_D, WCOL, C), F32),
        pltpu.VMEM((ROWS_D * HALF, C), F32),
    ]
    params = (
        dw_kernel, row(dw_bias), row(ln_gain), row(ln_bias), w_up, row(b_up), w_down, row(b_down),
        row(layer_scale),
    )
    cost = dict(flops=10**9, nbytes=4_000_000, trans=150_000)
    out_right, d_right, *stats_right, sums_right = call(
        right_half_kernel, half_outs, tiles, mixed, masked, above, below, *params,
        scratch=half_scratch, smem=(0,), **cost,
    )
    out_left, d_left, *stats_left, sums_left, win, send = call(
        left_half_kernel, half_outs + [((ROWS_D, WCOL, C), BF16), ((LEFT, C), BF16)],
        ends, tiles, mixed, got, masked, above, below, *params,
        scratch=half_scratch + [pltpu.VMEM((LEFT, C), F32)], smem=(0, 1), **cost,
    )

    flags = jnp.stack([lax.axis_index("c"), ends[0]])
    order = jnp.asarray(up_order(), BF16)
    record = ((N_X, REC, 128), BF16)
    mine, other = call(
        gradient_kernel, [record, record],
        flags, order, win, *stats_left, d_left, sums_left, *stats_right, d_right, sums_right,
        scratch=[
            pltpu.VMEM((ROWS_D, WCOL, C), F32),
            pltpu.VMEM((TILES_L, HID, 128), F32),
            pltpu.VMEM((8 * SMALL, 128), F32),
        ],
        smem=(0,), flops=2 * 10**9, nbytes=4_000_000,
    )
    got = lax.ppermute(other, "c", [(0, 1), (1, 0)])
    (part,) = call(core_sum_kernel, [record], mine, got, nbytes=3_000_000)
    part = lax.all_to_all(part, "x", 0, 0, tiled=True)
    part, send = call(
        spread_kernel, [((N_YZ, 16 + SMALL, 128), BF16), ((LEFT, C), BF16)], part, send,
        scratch=[pltpu.VMEM((REC, 128), F32)], nbytes=2_000_000,
    )
    part = lax.all_to_all(part, YZ, 0, 0, tiled=True)
    got = lax.ppermute(send, COL, [(i, (i - 1) % n_col) for i in range(n_col)])
    share, small = call(
        gather_kernel, [((16, 128), F32), ((N_X * N_C, SMALL, 128), F32)], part, nbytes=800_000
    )
    small = lax.all_to_all(small, CX, 0, 0, tiled=True)
    vectors = call(
        final_kernel, [((49, C), F32)] + [((C,), F32)] * 5 + [((HID,), F32)],
        small.reshape(-1, 128), nbytes=200_000,
    )
    shares = share.reshape(2, 8 * 128)
    shares = jnp.where(lax.axis_index("yh") == 0, shares[:, :SHARE], shares[:, 8 * 128 - SHARE :])
    grad_mixed, output = call(
        finish_kernel, [((PIX, C), F32), ((PIX, C), BF16)],
        ends, share, d_left, d_right, out_left, out_right, got, cot, dw_kernel,
        scratch=[pltpu.VMEM((ROWS_D, WCOL, C), F32)], smem=(0,), fence=(1,), flops=10**7, nbytes=1_000_000,
    )
    bias, gain, shift, b_down_grad, scale_grad, b_up_grad = vectors[1:]
    return (
        output.reshape(HB, WB, C), grad_mixed.reshape(HB, WB, C), shares[0], shares[1],
        vectors[0], bias, gain, shift, b_up_grad, b_down_grad, scale_grad,
    )


def solution(mesh):
    mesh = Mesh(mesh.devices.reshape(N_YL, N_X, N_C, N_Z, N_YH), ROW + COL)
    block = P(ROW, COL, None)
    in_specs = (block,) + (P(),) * 14 + (block, block)
    out_specs = (block, block, P(ROW + COL), P(ROW + COL)) + (P(),) * 7
    return jax.shard_map(body, mesh=mesh, in_specs=in_specs, out_specs=out_specs, check_vma=False)
```

```python
import numpy as np
import jax
import jax.numpy as jnp
from jax import lax
from jax.experimental import pallas as pl
from jax.experimental.pallas import tpu as pltpu
from jax.sharding import Mesh, PartitionSpec as P

ROW = ("yl", "x", "c")
COL = ("z", "yh")
YZ = ("yl", "z", "yh")
CX = ("c", "x")

F32 = jnp.float32
BF16 = jnp.bfloat16
EPS_NORM = 1e-06
GELU_SCALE = 0.7978845608028654
TS = 4
HB = 8
WB = 16
PIX = HB * WB
C = 384
HID = 1280
HEADS = 6
TILES_L = C // 128
N_YL, N_X, N_C, N_Z, N_YH = 4, 4, 2, 8, 2
N_ROW = N_YL * N_X * N_C
N_YZ = N_YL * N_Z * N_YH
SHARE = 960
SMALL = 24
REC = 1056
WCOL = 32
TILES = 8
HALO = 3
ROWS_M = HB + 4 * HALO
ROWS_D = HB + 2 * HALO
RIGHT_COT = 2 * HALO * ROWS_M
RIGHT_HIT = RIGHT_COT + HALO * ROWS_D
RIGHT = 176
LEFT_OUT = 2 * HALO * ROWS_D
LEFT = 112
HALF = WB // 2
PIX_H = HB * HALF
OWN = slice(HALO * HALF, HALO * HALF + PIX_H)

UP_TILES = (
    [(0, t) for t in range(8)],
    [(0, 7), (0, 8), (0, 9)] + [(1, t) for t in range(5)],
    [(1, t) for t in range(5, 10)] + [(2, t) for t in range(3)],
    [(2, t) for t in range(2, 10)],
)
DOWN_TILES = (
    [(0, t) for t in range(3)] + [(1, t) for t in range(3)] + [(2, 0), (2, 1)],
    [(2, 1), (2, 2)] + [(3, t) for t in range(3)] + [(4, t) for t in range(3)],
)


def call(
    kernel, outs, *args, scratch=(), smem=(), fence=(), hbm=(), flops=0, nbytes=0, trans=0, vmem=16
):
    n_in, n_out, n_scratch = len(args), len(outs), len(scratch)

    def run(*refs):
        targets = list(refs[n_in : n_in + n_out])
        extra = refs[n_in + n_out + n_scratch :]
        copies = []
        for j, i in enumerate(hbm):
            copies.append(pltpu.make_async_copy(extra[2 * j], targets[i], extra[2 * j + 1]))
            targets[i] = extra[2 * j]
        kernel(*refs[:n_in], *targets, *refs[n_in + n_out : n_in + n_out + n_scratch])
        for copy in copies:
            copy.start()
        for copy in copies:
            copy.wait()

    specs = [
        pl.BlockSpec(
            memory_space=pltpu.SMEM if i in smem else pl.ANY if i in fence else pltpu.VMEM
        )
        for i in range(n_in)
    ]
    buffers = [b for i in hbm for b in (pltpu.VMEM(*outs[i]), pltpu.SemaphoreType.DMA(()))]
    return pl.pallas_call(
        run,
        out_shape=[jax.ShapeDtypeStruct(s, d) for s, d in outs],
        in_specs=specs,
        out_specs=[
            pl.BlockSpec(memory_space=pltpu.HBM if i in hbm else pltpu.VMEM) for i in range(n_out)
        ],
        scratch_shapes=list(scratch) + buffers,
        compiler_params=pltpu.CompilerParams(vmem_limit_bytes=vmem * 1024 * 1024),
        cost_estimate=pl.CostEstimate(flops=flops, bytes_accessed=nbytes, transcendentals=trans),
    )(*args)


def mm(a, b, dims=((1,), (0,))):
    return lax.dot_general(a, b, (dims, ((), ())), preferred_element_type=F32)


def head_scaled(values):
    block = lax.broadcasted_iota(jnp.int32, (C, C), 0) // 64
    same = (block == lax.broadcasted_iota(jnp.int32, (C, C), 1) // 64).astype(F32).astype(BF16)
    squares = values * values
    high = squares.astype(BF16)
    low = (squares - high.astype(F32)).astype(BF16)
    return values * lax.rsqrt(mm(high, same) + mm(low, same) + EPS_NORM)


def pool_kernel(feat, out):
    total = feat[0].astype(F32)
    for r in range(1, HB):
        total = total + feat[r].astype(F32)
    mean = (total * (1.0 / HB)).astype(BF16)
    for i in range(N_ROW):
        out[i] = mean


def prepare_kernel(tiles, after, feat, cot, masked, first, last):
    pixel = lax.broadcasted_iota(jnp.int32, (PIX, 1), 0)
    value = (cot[...].astype(F32) * occupied(tiles, pixel // WB, pixel % WB)).astype(BF16)
    masked[...] = value
    n = 2 * HALO * WB
    m = HALO * WB
    first[:n, :] = feat[:n, :]
    first[n:, :] = value[:m]
    last[:n, :] = feat[PIX - n :, :]
    last[n:, :] = value[PIX - m :]


def occupied(tiles, row, col):
    tile = (row // TS) * (WB // TS) + col // TS
    weight = jnp.zeros(tile.shape, F32)
    for i in range(TILES):
        weight = jnp.where(tile == tiles[i], 1.0, weight)
    return weight


def split_columns(rows):
    shaped = rows.reshape(rows.shape[0] // WB, 2, WB // 2, rows.shape[1])
    return [shaped[:, h].reshape(-1, rows.shape[1]) for h in range(2)]


def stacked_rows(feat, above, below):
    n = 2 * HALO * WB
    return jnp.concatenate([above[:n, :], feat[...], below[:n, :]], axis=0)


def query_kernel(feat, above, below, w_query, out):
    query = head_scaled(mm(stacked_rows(feat, above, below), w_query[...]))
    for h, half in enumerate(split_columns(query)):
        out[h] = half.astype(BF16)


def right_attention_kernel(
    scale, valid, pooled, query, feat, above, below, w_key, w_value, w_out, tiles, masked,
    mixed, send, cot_grid, edges,
):
    out = attention(1, scale, valid, pooled, query, feat, above, below, w_key, w_value, w_out)
    mixed[...] = out.astype(BF16)
    cot_grid[...] = cot_rows(masked, above, below).astype(F32).reshape(ROWS_D, WB, C)
    edges[...] = jnp.zeros_like(edges)
    for r in range(ROWS_M):
        edges[6 * r : 6 * r + 6, :] = out[HALF * r + HALF - 6 : HALF * r + HALF]
    for r in range(ROWS_D):
        at = RIGHT_COT + HALO * r
        edges[at : at + HALO, :] = cot_grid[r, WB - HALO :, :]
    tile_row = lax.broadcasted_iota(jnp.int32, (1, C), 1) // 128 * TS
    edges[RIGHT_HIT : RIGHT_HIT + 1, :] = occupied(tiles, tile_row, jnp.full((1, C), WB - 1))
    send[...] = edges[...].astype(BF16)


def left_attention_kernel(
    scale, valid, pooled, query, feat, above, below, w_key, w_value, w_out, after, mixed
):
    out = attention(0, scale, valid, pooled, query, feat, above, below, w_key, w_value, w_out)
    mixed[...] = out.astype(BF16)


def attention(h, scale, valid, pooled, query, feat, above, below, w_key, w_value, w_out):
    rows = split_columns(pooled[...].astype(F32))[h].astype(BF16)
    keys = head_scaled(mm(rows, w_key[...])).astype(BF16)
    values = mm(rows, w_value[...]).astype(BF16)
    half_feat = split_columns(stacked_rows(feat, above, below).astype(F32))[h]
    n_query, n_keys = ROWS_M * HALF, N_ROW * HALF
    same = (
        lax.broadcasted_iota(jnp.int32, (n_query, n_keys), 0) % HALF
        == lax.broadcasted_iota(jnp.int32, (n_query, n_keys), 1) % HALF
    )
    lower = lax.broadcasted_iota(jnp.int32, (n_query, 128), 1) < 64
    row = lax.broadcasted_iota(jnp.int32, (n_query, 1), 0) // HALF
    inside = ((row >= 2 * HALO) | (valid[0] > 0)) & ((row < 2 * HALO + HB) | (valid[1] > 0))
    pairs = []
    for pair in range(HEADS // 2):
        lanes = slice(128 * pair, 128 * pair + 128)
        q = query[h, :, lanes].astype(F32)
        parts = []
        for sub in range(2):
            q_half = jnp.where(lower if sub == 0 else ~lower, q, 0.0).astype(BF16)
            scores = mm(q_half, keys[:, lanes], ((1,), (1,)))
            weight = jnp.where(same, jnp.exp(scores * scale[2 * pair + sub]), 0.0)
            total = jnp.sum(weight, axis=1, keepdims=True)
            parts.append(mm(weight.astype(BF16), values[:, lanes]) / total)
        pairs.append(jnp.where(lower, parts[0], parts[1]).astype(BF16))
    attended = jnp.concatenate(pairs, axis=1)
    return jnp.where(inside, half_feat + mm(attended, w_out[...]), 0.0)


def cot_rows(masked, above, below):
    n = 2 * HALO * WB
    return jnp.concatenate([above[n:, :], masked[...], below[n:, :]], axis=0)


def border_mask(is_first, dj, start, size):
    u = lax.broadcasted_iota(jnp.int32, (size, 128), 0) + start
    crosses = (u < HALO) != (u + dj < 2 * HALO)
    return jnp.where(crosses & is_first, 0.0, 1.0)


def depthwise(win, taps, n_out, base, halves, start, flip, store, is_first=None):
    masks = [None] * 7
    if is_first is not None:
        masks = [border_mask(is_first, dj, 0, HALF) for dj in range(7)]
    for t in range(TILES_L):
        lanes = slice(128 * t, 128 * t + 128)
        for h in halves:
            acc = [start(r, h, lanes) for r in range(n_out)]
            for dj in range(7):
                at = base + HALF * h + dj
                cols = [win[r, at : at + HALF, lanes] for r in range(n_out + 6)]
                if h == 0 and dj != 3 and is_first is not None:
                    cols = [col * masks[dj] for col in cols]
                for di in range(7):
                    tap = 7 * di + dj if not flip else 7 * (6 - di) + (6 - dj)
                    k = taps[tap : tap + 1, lanes]
                    for r in range(n_out):
                        acc[r] = acc[r] + cols[r + di] * k
            for r in range(n_out):
                store(r, h, lanes, acc[r])


def rowsum(a):
    return jnp.sum(a, axis=0, keepdims=True)


def right_half_kernel(tiles, mixed_left, mixed_right, masked, above, below, *refs):
    sublayer(1, None, tiles, mixed_left, mixed_right, None, masked, above, below, *refs)


def left_half_kernel(at_first, tiles, mixed_left, mixed_right, got, masked, above, below, *refs):
    sublayer(0, at_first, tiles, mixed_left, mixed_right, got, masked, above, below, *refs)


def sublayer(
    h, at_first, tiles, mixed_left, mixed_right, got, masked, above, below, taps, dw_bias, ln_gain,
    ln_bias, w_up, b_up, w_down, b_down, layer_scale, output, d_out, lnout_out, hidden_out,
    d_pre_out, d_branch_out, sums, tap_sums, *refs,
):
    is_first = None
    if h == 0:
        send, win, grid, spat, edges = refs
        is_first = at_first[0] > 0
        halo = got[...].astype(F32)
    else:
        win, grid, spat = refs
    for i, mixed in enumerate((mixed_left, mixed_right)):
        values = mixed[...].astype(F32)
        for r in range(ROWS_M):
            win[r, 8 + HALF * i : 8 + HALF * i + HALF, :] = values[r * HALF : (r + 1) * HALF]
    if h == 0:
        for r in range(ROWS_M):
            win[r, 2:8, :] = halo[6 * r : 6 * r + 6]
    grid[:, 8 : 8 + WB, :] = cot_rows(masked, above, below).astype(F32).reshape(ROWS_D, WB, C)
    pixel = lax.broadcasted_iota(jnp.int32, (PIX_H, 1), 0)
    row, col = pixel // HALF, pixel % HALF + HALF * h - HALO
    weight = occupied(tiles, row, jnp.maximum(col, 0))
    if h == 0:
        for r in range(ROWS_D):
            at = RIGHT_COT + HALO * r
            grid[r, 8 - HALO : 8, :] = halo[at : at + HALO]
        hits = halo[RIGHT_HIT : RIGHT_HIT + 1]
        before = jnp.where(row < TS, hits[:, 0:1], hits[:, 128:129])
        weight = jnp.where(col < 0, before, weight)
    here = slice(8 - HALO + HALF * h, 8 - HALO + HALF * h + HALF)
    cotan = grid[:, here, :].reshape(ROWS_D * HALF, C)

    def start(r, h, lanes):
        return jnp.broadcast_to(dw_bias[:, lanes], (HALF, 128))

    def store(r, h, lanes, value):
        spat[r * HALF : (r + 1) * HALF, lanes] = value

    depthwise(win, taps, ROWS_D, 2, (h,), start, False, store, is_first)
    spatial = spat[...]
    center = spatial - jnp.mean(spatial, axis=1, keepdims=True)
    inv_std = lax.rsqrt(jnp.mean(center * center, axis=1, keepdims=True) + EPS_NORM)
    standard = center * inv_std
    gain = ln_gain[...]
    lnout = (standard * gain + ln_bias[...]).astype(BF16)
    lnout_out[...] = lnout[OWN]
    preact = mm(lnout, w_up[...]) + b_up[...]
    square = 0.044715 * preact * preact
    tanh_val = jnp.tanh(GELU_SCALE * preact * (1.0 + square))
    hidden = (0.5 * preact[OWN] * (1.0 + tanh_val[OWN])).astype(BF16)
    slope = 0.5 * (1.0 + tanh_val) + 0.5 * preact * (1.0 - tanh_val * tanh_val) * GELU_SCALE * (
        1.0 + 3.0 * square
    )
    hidden_out[...] = hidden
    scale = layer_scale[...]
    d_branch = cotan * scale
    d_branch_b = d_branch.astype(BF16)
    d_branch_out[...] = d_branch_b[OWN]
    d_pre = mm(d_branch_b, w_down[...], ((1,), (1,))) * slope
    d_pre_b = d_pre.astype(BF16)
    d_pre_out[...] = d_pre_b[OWN]
    d_lnout = mm(d_pre_b, w_up[...], ((1,), (1,)))
    e = d_lnout * gain
    d_spatial = inv_std * (
        e
        - jnp.mean(e, axis=1, keepdims=True)
        - standard * jnp.mean(e * standard, axis=1, keepdims=True)
    )
    d_out[...] = d_spatial
    branch = (mm(hidden, w_down[...]) + b_down[...]) * weight
    base = win[2 * HALO : 2 * HALO + HB, here, :].reshape(PIX_H, C)
    out = base + scale * branch
    output[...] = out.astype(BF16)
    if h == 0:
        edges[...] = jnp.zeros_like(edges)
        for r in range(ROWS_D):
            edges[6 * r : 6 * r + 6, :] = d_spatial[r * HALF : r * HALF + 6]
        for r in range(HB):
            at = LEFT_OUT + HALO * r
            edges[at : at + HALO, :] = out[r * HALF : r * HALF + HALO]
        send[...] = edges[...].astype(BF16)
    d_lnout = d_lnout[OWN]
    sums[0:1, :C] = rowsum(d_spatial[OWN])
    sums[1:2, :C] = rowsum(d_lnout * standard[OWN])
    sums[2:3, :C] = rowsum(d_lnout)
    sums[3:4, :C] = rowsum(d_branch[OWN])
    sums[4:5, :C] = rowsum(cotan[OWN] * branch)
    sums[5:6, :] = rowsum(d_pre[OWN])
    tap_sums[...] = jnp.zeros_like(tap_sums)
    for t in range(TILES_L):
        lanes = slice(128 * t, 128 * t + 128)
        d_rows = [
            d_spatial[(HALO + r) * HALF : (HALO + r + 1) * HALF, lanes] for r in range(HB)
        ]
        for dj in range(7):
            at = 2 + HALF * h + dj
            cols = [win[HALO + r, at : at + HALF, lanes] for r in range(ROWS_D)]
            if h == 0 and dj != 3:
                mask = border_mask(is_first, dj, 0, HALF)
                cols = [col * mask for col in cols]
            for di in range(7):
                acc = cols[di] * d_rows[0]
                for r in range(1, HB):
                    acc = acc + cols[r + di] * d_rows[r]
                row = 56 * t + 7 * di + dj
                tap_sums[row : row + 1, :] = rowsum(acc)


def up_order():
    chan = np.arange(C).reshape(N_YL, N_X, N_C, N_Z // 2, 3).transpose(4, 2, 1, 0, 3).reshape(-1)
    return (np.arange(C)[:, None] == chan[None, :]).astype(np.float32)


def gradient_kernel(
    core, order, *refs
):
    halves = [refs[:6], refs[6:12]]
    mine, other, down, small = refs[12:]
    lnout, hidden, d_pre, d_branch = [
        jnp.concatenate([halves[0][i][...], halves[1][i][...]], axis=0) for i in range(4)
    ]
    is_zero = core[0] == 0

    def put(row, x, zero, one):
        size = zero.shape[0]
        mine[x, row : row + size, :] = jnp.where(is_zero, zero, one).astype(BF16)
        other[x, row : row + size, :] = jnp.where(is_zero, one, zero).astype(BF16)

    ordered = mm(lnout, order[...]).astype(BF16)
    ups = [mm(ordered[:, 128 * r : 128 * r + 128], d_pre, ((0,), (0,))) for r in range(3)]
    for q in range(4):
        for k, (r, t) in enumerate(UP_TILES[q]):
            for x in range(N_X):
                pair = [ups[r][64 * c + 16 * x : 64 * c + 16 * x + 16, 128 * t : 128 * t + 128] for c in range(2)]
                put((q * 8 + k) * 16, x, *pair)
    full = mm(hidden, d_branch, ((0,), (0,)))
    for t in range(TILES_L):
        down[t] = full[:, 128 * t : 128 * t + 128]
    for yh in range(2):
        for k, (s, t) in enumerate(DOWN_TILES[yh]):
            for x in range(N_X):
                for two in range(2):
                    pair = [
                        jnp.concatenate(
                            [
                                down[t, pl.ds(5 * (64 * yl + 16 * x + 8 * c) + s, 8, stride=5), :]
                                for yl in (2 * two, 2 * two + 1)
                            ],
                            axis=0,
                        )
                        for c in range(2)
                    ]
                    put(512 + (yh * 8 + k) * 32 + 16 * two, x, *pair)
    small[...] = jnp.zeros_like(small)
    small[:168, :] = halves[0][4][...] + halves[1][4][...]
    sums = halves[0][5][...] + halves[1][5][...]
    for i in range(5):
        for t in range(TILES_L):
            small[161 + 3 * i + t : 162 + 3 * i + t, :] = sums[i : i + 1, 128 * t : 128 * t + 128]
    for t in range(HID // 128):
        small[176 + t : 177 + t, :] = sums[5:6, 128 * t : 128 * t + 128]
    for x in range(N_X):
        pair = [
            jnp.concatenate([small[96 * c + 24 * x : 96 * c + 24 * x + 24], jnp.zeros((8, 128), F32)], axis=0)
            for c in range(2)
        ]
        put(1024, x, *pair)


def spread_kernel(part, after, out, total):
    total[...] = (
        (part[0].astype(F32) + part[1].astype(F32)) + (part[2].astype(F32) + part[3].astype(F32))
    )
    small = total[1024 : 1024 + SMALL, :]
    for yl in range(N_YL):
        for z in range(N_Z):
            for yh in range(N_YH):
                q = (z % 2) * 2 + yh
                up = total[pl.ds(q * 128 + yl * 4 + z // 2, 8, stride=16), :]
                down = total[pl.ds(512 + yh * 256 + yl * 8 + z, 8, stride=32), :]
                record = jnp.concatenate([up, down, small], axis=0)
                out[(yl * N_Z + z) * N_YH + yh] = record.astype(BF16)


def gather_kernel(part, share, small):
    total = part[0].astype(F32)
    for i in range(1, N_YZ):
        total = total + part[i].astype(F32)
    share[...] = total[:16]
    for i in range(N_X * N_C):
        small[i] = total[16:]


def final_kernel(small, dw, *vectors):
    for t in range(TILES_L):
        dw[:, 128 * t : 128 * t + 128] = small[56 * t : 56 * t + 49, :]
    for i in range(5):
        for t in range(TILES_L):
            vectors[i][pl.ds(128 * t, 128)] = small[161 + 3 * i + t, :]
    for t in range(HID // 128):
        vectors[5][pl.ds(128 * t, 128)] = small[176 + t, :]


def finish_kernel(
    at_ends, after, d_left, d_right, out_left, out_right, got, cot, taps, grad, output, win
):
    halo = got[...].astype(F32)
    column = lax.broadcasted_iota(jnp.int32, (HALF, 1), 0)
    here = jnp.where((column < HALO) & (at_ends[0] > 0), 0.0, 1.0)
    beyond = lax.broadcasted_iota(jnp.int32, (6, 1), 0)
    there = jnp.where((beyond >= HALO) & (at_ends[1] > 0), 0.0, 1.0)
    for r in range(HB):
        at = LEFT_OUT + HALO * r
        win[r, 8 : 8 + HALF, :] = out_left[r * HALF : (r + 1) * HALF, :].astype(F32)
        win[r, 8 + HALF : 8 + WB, :] = out_right[r * HALF : (r + 1) * HALF, :].astype(F32)
        win[r, 8 + WB : 8 + WB + HALO, :] = halo[at : at + HALO]
    output[...] = win[:HB, 8 + HALO : 8 + HALO + WB, :].reshape(PIX, C).astype(BF16)
    for r in range(ROWS_D):
        win[r, 8 : 8 + HALF, :] = d_left[r * HALF : (r + 1) * HALF, :] * here
        win[r, 8 + HALF : 8 + WB, :] = d_right[r * HALF : (r + 1) * HALF, :]
        win[r, 8 + WB : 14 + WB, :] = halo[6 * r : 6 * r + 6] * there

    def start(r, h, lanes):
        return cot[r * WB : (r + 1) * WB, lanes].astype(F32)[HALF * h : HALF * h + HALF]

    def store(r, h, lanes, value):
        at = r * WB + HALF * h
        grad[at : at + HALF, lanes] = value

    depthwise(win, taps, HB, 8, (0, 1), start, True, store)


def core_sum_kernel(mine, got, send, out, send_out):
    send_out[...] = send[...]
    out[...] = (mine[...].astype(F32) + got[...].astype(F32)).astype(BF16)


def neighbours(before_edge, after_edge, axes):
    size = lax.axis_size(axes)
    up = [(i, i + 1) for i in range(size - 1)]
    down = [(i + 1, i) for i in range(size - 1)]
    return lax.ppermute(after_edge, axes, up), lax.ppermute(before_edge, axes, down)


def body(
    features, w_query, w_key, w_value, w_out, logit_scale, dw_kernel, dw_bias, ln_gain, ln_bias,
    w_up, b_up, w_down, b_down, layer_scale, cotangent, tile_list,
):
    row = lambda v: v.reshape(1, -1)
    flat = features.reshape(PIX, C)
    cot = cotangent.reshape(PIX, C)

    (copies,) = call(pool_kernel, [((N_ROW, WB, C), BF16)], features, nbytes=500_000)
    pooled = lax.all_to_all(copies, ROW, 0, 0, tiled=True).reshape(N_ROW * WB, C)

    shared = ((3 * HALO * WB, C), BF16)
    tiles = tile_list.reshape(-1)
    masked, feat_first, feat_last = call(
        prepare_kernel, [((PIX, C), BF16), shared, shared],
        tiles, copies, flat, cot, smem=(0,), fence=(1,), nbytes=800_000,
    )
    above, below = neighbours(feat_first, feat_last, ROW)
    (query,) = call(
        query_kernel, [((2, ROWS_M * WB // 2, C), BF16)], flat, above, below, w_query,
        flops=2 * 10**8, nbytes=900_000,
    )
    at_row = lax.axis_index(ROW)
    valid = jnp.stack([at_row > 0, at_row < N_ROW - 1]).astype(jnp.int32)
    inputs = (logit_scale, valid, pooled, query, flat, above, below, w_key, w_value, w_out)
    half_mixed = ((ROWS_M * HALF, C), BF16)
    cost = dict(flops=5 * 10**8, nbytes=1_500_000, trans=250_000)
    mixed_right, send = call(
        right_attention_kernel, [half_mixed, ((RIGHT, C), BF16)], *inputs, tiles, masked,
        scratch=[pltpu.VMEM((ROWS_D, WB, C), F32), pltpu.VMEM((RIGHT, C), F32)],
        smem=(0, 1, 10), **cost,
    )
    n_col = lax.axis_size(COL)
    at_col = lax.axis_index(COL)
    got = lax.ppermute(send, COL, [(i, (i + 1) % n_col) for i in range(n_col)])
    (mixed_left,) = call(
        left_attention_kernel, [half_mixed], *inputs, mixed_right, smem=(0, 1), fence=(10,), **cost
    )
    ends = jnp.stack([at_col == 0, at_col == n_col - 1]).astype(jnp.int32)

    half_outs = [
        ((PIX_H, C), BF16), ((ROWS_D * HALF, C), F32), ((PIX_H, C), BF16), ((PIX_H, HID), BF16),
        ((PIX_H, HID), BF16), ((PIX_H, C), BF16), ((8, HID), F32), ((168, 128), F32),
    ]
    half_scratch = [
        pltpu.VMEM((ROWS_M, WCOL, C), F32), pltpu.VMEM((ROWS_D, WCOL, C), F32),
        pltpu.VMEM((ROWS_D * HALF, C), F32),
    ]
    params = (
        dw_kernel, row(dw_bias), row(ln_gain), row(ln_bias), w_up, row(b_up), w_down, row(b_down),
        row(layer_scale),
    )
    cost = dict(flops=10**9, nbytes=4_000_000, trans=150_000)
    out_right, d_right, *stats_right, sums_right, taps_right = call(
        right_half_kernel, half_outs, tiles, mixed_left, mixed_right, masked, above, below, *params,
        scratch=half_scratch, smem=(0,), **cost,
    )
    out_left, d_left, *stats_left, sums_left, taps_left, send = call(
        left_half_kernel, half_outs + [((LEFT, C), BF16)],
        ends, tiles, mixed_left, mixed_right, got, masked, above, below, *params,
        scratch=half_scratch + [pltpu.VMEM((LEFT, C), F32)], smem=(0, 1), **cost,
    )

    core = lax.axis_index("c").reshape(1)
    order = jnp.asarray(up_order(), BF16)
    record = ((N_X, REC, 128), BF16)
    mine, other = call(
        gradient_kernel, [record, record],
        core, order, *stats_left, taps_left, sums_left, *stats_right, taps_right, sums_right,
        scratch=[
            pltpu.VMEM((TILES_L, HID, 128), F32),
            pltpu.VMEM((8 * SMALL, 128), F32),
        ],
        smem=(0,), flops=2 * 10**9, nbytes=4_000_000,
    )
    got = lax.ppermute(other, "c", [(0, 1), (1, 0)])
    part, send = call(
        core_sum_kernel, [record, ((LEFT, C), BF16)], mine, got, send, nbytes=3_000_000
    )
    part = lax.all_to_all(part, "x", 0, 0, tiled=True)
    got = lax.ppermute(send, COL, [(i, (i - 1) % n_col) for i in range(n_col)])
    (spread,) = call(
        spread_kernel, [((N_YZ, 16 + SMALL, 128), BF16)], part, got, fence=(1,),
        scratch=[pltpu.VMEM((REC, 128), F32)], hbm=(0,), nbytes=2_000_000,
    )
    part = lax.all_to_all(spread, YZ, 0, 0, tiled=True)
    share, small = call(
        gather_kernel, [((16, 128), F32), ((N_X * N_C, SMALL, 128), F32)], part, nbytes=800_000
    )
    small = lax.all_to_all(small, CX, 0, 0, tiled=True)
    vectors = call(
        final_kernel, [((49, C), F32)] + [((C,), F32)] * 5 + [((HID,), F32)],
        small.reshape(-1, 128), nbytes=200_000,
    )
    shares = share.reshape(2, 8 * 128)
    shares = jnp.where(lax.axis_index("yh") == 0, shares[:, :SHARE], shares[:, 8 * 128 - SHARE :])
    grad_mixed, output = call(
        finish_kernel, [((PIX, C), F32), ((PIX, C), BF16)],
        ends, spread, d_left, d_right, out_left, out_right, got, cot, dw_kernel,
        scratch=[pltpu.VMEM((ROWS_D, WCOL, C), F32)], smem=(0,), fence=(1,), flops=10**7, nbytes=1_000_000,
    )
    bias, gain, shift, b_down_grad, scale_grad, b_up_grad = vectors[1:]
    return (
        output.reshape(HB, WB, C), grad_mixed.reshape(HB, WB, C), shares[0], shares[1],
        vectors[0], bias, gain, shift, b_up_grad, b_down_grad, scale_grad,
    )


def solution(mesh):
    mesh = Mesh(mesh.devices.reshape(N_YL, N_X, N_C, N_Z, N_YH), ROW + COL)
    block = P(ROW, COL, None)
    in_specs = (block,) + (P(),) * 14 + (block, block)
    out_specs = (block, block, P(ROW + COL), P(ROW + COL)) + (P(),) * 7
    return jax.shard_map(body, mesh=mesh, in_specs=in_specs, out_specs=out_specs, check_vma=False)
```

```python
import numpy as np
import jax
import jax.numpy as jnp
from jax import lax
from jax.experimental import pallas as pl
from jax.experimental.pallas import tpu as pltpu
from jax.sharding import Mesh, PartitionSpec as P

ROW = ("yl", "x", "c")
COL = ("z", "yh")
YZ = ("yl", "z", "yh")
CX = ("c", "x")

F32 = jnp.float32
BF16 = jnp.bfloat16
EPS_NORM = 1e-06
GELU_SCALE = 0.7978845608028654
TS = 4
HB = 8
WB = 16
PIX = HB * WB
C = 384
HID = 1280
HEADS = 6
TILES_L = C // 128
N_YL, N_X, N_C, N_Z, N_YH = 4, 4, 2, 8, 2
N_ROW = N_YL * N_X * N_C
N_YZ = N_YL * N_Z * N_YH
SHARE = 960
SMALL = 24
REC = 1056
WCOL = 32
TILES = 8
HALO = 3
ROWS_M = HB + 4 * HALO
ROWS_D = HB + 2 * HALO
RIGHT_COT = 2 * HALO * ROWS_M
RIGHT_HIT = RIGHT_COT + HALO * ROWS_D
RIGHT = 176
LEFT_OUT = 2 * HALO * ROWS_D
LEFT = 112
HALF = WB // 2
PIX_H = HB * HALF
OWN = slice(HALO * HALF, HALO * HALF + PIX_H)

UP_TILES = (
    [(0, t) for t in range(8)],
    [(0, 7), (0, 8), (0, 9)] + [(1, t) for t in range(5)],
    [(1, t) for t in range(5, 10)] + [(2, t) for t in range(3)],
    [(2, t) for t in range(2, 10)],
)
DOWN_TILES = (
    [(0, t) for t in range(3)] + [(1, t) for t in range(3)] + [(2, 0), (2, 1)],
    [(2, 1), (2, 2)] + [(3, t) for t in range(3)] + [(4, t) for t in range(3)],
)


def call(
    kernel, outs, *args, scratch=(), smem=(), fence=(), hbm=(), own=(), flops=0, nbytes=0, trans=0, vmem=16
):
    n_in, n_out, n_scratch = len(args), len(outs), len(scratch)

    def run(*refs):
        targets = list(refs[n_in : n_in + n_out])
        extra = refs[n_in + n_out + n_scratch :]
        copies = []
        for j, i in enumerate(hbm):
            copies.append(pltpu.make_async_copy(extra[2 * j], targets[i], extra[2 * j + 1]))
            targets[i] = extra[2 * j]
        kernel(*refs[:n_in], *targets, *refs[n_in + n_out : n_in + n_out + n_scratch])
        for copy in copies:
            copy.start()
        for copy in copies:
            copy.wait()

    specs = [
        pl.BlockSpec(
            memory_space=pltpu.SMEM if i in smem else pl.ANY if i in fence else pltpu.VMEM
        )
        for i in range(n_in)
    ]
    buffers = [b for i in hbm for b in (pltpu.VMEM(*outs[i]), pltpu.SemaphoreType.DMA(()))]
    return pl.pallas_call(
        run,
        out_shape=[jax.ShapeDtypeStruct(s, d) for s, d in outs],
        in_specs=specs,
        out_specs=[
            pl.BlockSpec(memory_space=pltpu.HBM if i in hbm or i in own else pltpu.VMEM) for i in range(n_out)
        ],
        scratch_shapes=list(scratch) + buffers,
        compiler_params=pltpu.CompilerParams(vmem_limit_bytes=vmem * 1024 * 1024),
        cost_estimate=pl.CostEstimate(flops=flops, bytes_accessed=nbytes, transcendentals=trans),
    )(*args)


def mm(a, b, dims=((1,), (0,))):
    return lax.dot_general(a, b, (dims, ((), ())), preferred_element_type=F32)


def head_scaled(values):
    block = lax.broadcasted_iota(jnp.int32, (C, C), 0) // 64
    same = (block == lax.broadcasted_iota(jnp.int32, (C, C), 1) // 64).astype(F32).astype(BF16)
    squares = values * values
    high = squares.astype(BF16)
    low = (squares - high.astype(F32)).astype(BF16)
    return values * lax.rsqrt(mm(high, same) + mm(low, same) + EPS_NORM)


def pool_kernel(feat, out):
    total = feat[0].astype(F32)
    for r in range(1, HB):
        total = total + feat[r].astype(F32)
    mean = (total * (1.0 / HB)).astype(BF16)
    for i in range(N_ROW):
        out[i] = mean


def prepare_kernel(tiles, after, feat, cot, masked, first, last):
    pixel = lax.broadcasted_iota(jnp.int32, (PIX, 1), 0)
    value = (cot[...].astype(F32) * occupied(tiles, pixel // WB, pixel % WB)).astype(BF16)
    masked[...] = value
    n = 2 * HALO * WB
    m = HALO * WB
    first[:n, :] = feat[:n, :]
    first[n:, :] = value[:m]
    last[:n, :] = feat[PIX - n :, :]
    last[n:, :] = value[PIX - m :]


def occupied(tiles, row, col):
    tile = (row // TS) * (WB // TS) + col // TS
    weight = jnp.zeros(tile.shape, F32)
    for i in range(TILES):
        weight = jnp.where(tile == tiles[i], 1.0, weight)
    return weight


def split_columns(rows):
    shaped = rows.reshape(rows.shape[0] // WB, 2, WB // 2, rows.shape[1])
    return [shaped[:, h].reshape(-1, rows.shape[1]) for h in range(2)]


def stacked_rows(feat, above, below):
    n = 2 * HALO * WB
    return jnp.concatenate([above[:n, :], feat[...], below[:n, :]], axis=0)


def query_kernel(feat, above, below, w_query, out):
    query = head_scaled(mm(stacked_rows(feat, above, below), w_query[...]))
    for h, half in enumerate(split_columns(query)):
        out[h] = half.astype(BF16)


def right_attention_kernel(
    scale, valid, pooled, query, feat, above, below, w_key, w_value, w_out, tiles, masked,
    mixed, send, cot_grid, edges,
):
    out = attention(1, scale, valid, pooled, query, feat, above, below, w_key, w_value, w_out)
    mixed[...] = out.astype(BF16)
    cot_grid[...] = cot_rows(masked, above, below).astype(F32).reshape(ROWS_D, WB, C)
    edges[...] = jnp.zeros_like(edges)
    for r in range(ROWS_M):
        edges[6 * r : 6 * r + 6, :] = out[HALF * r + HALF - 6 : HALF * r + HALF]
    for r in range(ROWS_D):
        at = RIGHT_COT + HALO * r
        edges[at : at + HALO, :] = cot_grid[r, WB - HALO :, :]
    tile_row = lax.broadcasted_iota(jnp.int32, (1, C), 1) // 128 * TS
    edges[RIGHT_HIT : RIGHT_HIT + 1, :] = occupied(tiles, tile_row, jnp.full((1, C), WB - 1))
    send[...] = edges[...].astype(BF16)


def left_attention_kernel(
    scale, valid, pooled, query, feat, above, below, w_key, w_value, w_out, after, mixed
):
    out = attention(0, scale, valid, pooled, query, feat, above, below, w_key, w_value, w_out)
    mixed[...] = out.astype(BF16)


def attention(h, scale, valid, pooled, query, feat, above, below, w_key, w_value, w_out):
    rows = split_columns(pooled[...].astype(F32))[h].astype(BF16)
    keys = head_scaled(mm(rows, w_key[...])).astype(BF16)
    values = mm(rows, w_value[...]).astype(BF16)
    half_feat = split_columns(stacked_rows(feat, above, below).astype(F32))[h]
    n_query, n_keys = ROWS_M * HALF, N_ROW * HALF
    same = (
        lax.broadcasted_iota(jnp.int32, (n_query, n_keys), 0) % HALF
        == lax.broadcasted_iota(jnp.int32, (n_query, n_keys), 1) % HALF
    )
    lower = lax.broadcasted_iota(jnp.int32, (n_query, 128), 1) < 64
    row = lax.broadcasted_iota(jnp.int32, (n_query, 1), 0) // HALF
    inside = ((row >= 2 * HALO) | (valid[0] > 0)) & ((row < 2 * HALO + HB) | (valid[1] > 0))
    pairs = []
    for pair in range(HEADS // 2):
        lanes = slice(128 * pair, 128 * pair + 128)
        q = query[h, :, lanes].astype(F32)
        parts = []
        for sub in range(2):
            q_half = jnp.where(lower if sub == 0 else ~lower, q, 0.0).astype(BF16)
            scores = mm(q_half, keys[:, lanes], ((1,), (1,)))
            weight = jnp.where(same, jnp.exp(scores * scale[2 * pair + sub]), 0.0)
            total = jnp.sum(weight, axis=1, keepdims=True)
            parts.append(mm(weight.astype(BF16), values[:, lanes]) / total)
        pairs.append(jnp.where(lower, parts[0], parts[1]).astype(BF16))
    attended = jnp.concatenate(pairs, axis=1)
    return jnp.where(inside, half_feat + mm(attended, w_out[...]), 0.0)


def cot_rows(masked, above, below):
    n = 2 * HALO * WB
    return jnp.concatenate([above[n:, :], masked[...], below[n:, :]], axis=0)


def border_mask(is_first, dj, start, size):
    u = lax.broadcasted_iota(jnp.int32, (size, 128), 0) + start
    crosses = (u < HALO) != (u + dj < 2 * HALO)
    return jnp.where(crosses & is_first, 0.0, 1.0)


def eight_columns(win, rows, at, lanes):
    shift = at % 8
    low = [win[r, at - shift : at - shift + 8, lanes] for r in rows]
    if shift == 0:
        return low
    sub = lax.broadcasted_iota(jnp.int32, (8, 128), 0)
    high = [win[r, at - shift + 8 : at - shift + 16, lanes] for r in rows]
    return [
        pltpu.roll(jnp.where(sub < shift, b, a), 8 - shift, axis=0) for a, b in zip(low, high)
    ]


def depthwise(win, taps, n_out, base, halves, start, flip, store, is_first=None):
    masks = [None] * 7
    if is_first is not None:
        masks = [border_mask(is_first, dj, 0, HALF) for dj in range(7)]
    for t in range(TILES_L):
        lanes = slice(128 * t, 128 * t + 128)
        for h in halves:
            acc = [start(r, h, lanes) for r in range(n_out)]
            for dj in range(7):
                at = base + HALF * h + dj
                cols = eight_columns(win, range(n_out + 6), at, lanes)
                if h == 0 and dj != 3 and is_first is not None:
                    cols = [col * masks[dj] for col in cols]
                for di in range(7):
                    tap = 7 * di + dj if not flip else 7 * (6 - di) + (6 - dj)
                    k = taps[tap : tap + 1, lanes]
                    for r in range(n_out):
                        acc[r] = acc[r] + cols[r + di] * k
            for r in range(n_out):
                store(r, h, lanes, acc[r])


def rowsum(a):
    return jnp.sum(a, axis=0, keepdims=True)


def right_half_kernel(tiles, mixed_left, mixed_right, masked, above, below, *refs):
    sublayer(1, None, tiles, mixed_left, mixed_right, None, masked, above, below, *refs)


def left_half_kernel(at_first, tiles, mixed_left, mixed_right, got, masked, above, below, *refs):
    sublayer(0, at_first, tiles, mixed_left, mixed_right, got, masked, above, below, *refs)


def sublayer(
    h, at_first, tiles, mixed_left, mixed_right, got, masked, above, below, taps, dw_bias, ln_gain,
    ln_bias, w_up, b_up, w_down, b_down, layer_scale, output, d_out, lnout_out, hidden_out,
    d_pre_out, d_branch_out, sums, tap_sums, *refs,
):
    is_first = None
    if h == 0:
        send, win, grid, spat, edges = refs
        is_first = at_first[0] > 0
        halo = got[...].astype(F32)
    else:
        win, grid, spat = refs
    for i, mixed in enumerate((mixed_left, mixed_right)):
        values = mixed[...].astype(F32)
        for r in range(ROWS_M):
            win[r, 8 + HALF * i : 8 + HALF * i + HALF, :] = values[r * HALF : (r + 1) * HALF]
    if h == 0:
        for r in range(ROWS_M):
            win[r, 2:8, :] = halo[6 * r : 6 * r + 6]
    grid[:, 8 : 8 + WB, :] = cot_rows(masked, above, below).astype(F32).reshape(ROWS_D, WB, C)
    pixel = lax.broadcasted_iota(jnp.int32, (PIX_H, 1), 0)
    row, col = pixel // HALF, pixel % HALF + HALF * h - HALO
    weight = occupied(tiles, row, jnp.maximum(col, 0))
    if h == 0:
        for r in range(ROWS_D):
            at = RIGHT_COT + HALO * r
            grid[r, 8 - HALO : 8, :] = halo[at : at + HALO]
        hits = halo[RIGHT_HIT : RIGHT_HIT + 1]
        before = jnp.where(row < TS, hits[:, 0:1], hits[:, 128:129])
        weight = jnp.where(col < 0, before, weight)
    here = slice(8 - HALO + HALF * h, 8 - HALO + HALF * h + HALF)
    cotan = grid[:, here, :].reshape(ROWS_D * HALF, C)

    def start(r, h, lanes):
        return jnp.broadcast_to(dw_bias[:, lanes], (HALF, 128))

    def store(r, h, lanes, value):
        spat[r * HALF : (r + 1) * HALF, lanes] = value

    depthwise(win, taps, ROWS_D, 2, (h,), start, False, store, is_first)
    spatial = spat[...]
    center = spatial - jnp.mean(spatial, axis=1, keepdims=True)
    inv_std = lax.rsqrt(jnp.mean(center * center, axis=1, keepdims=True) + EPS_NORM)
    standard = center * inv_std
    gain = ln_gain[...]
    lnout = (standard * gain + ln_bias[...]).astype(BF16)
    lnout_out[...] = lnout[OWN]
    preact = mm(lnout, w_up[...]) + b_up[...]
    square = 0.044715 * preact * preact
    tanh_val = jnp.tanh(GELU_SCALE * preact * (1.0 + square))
    hidden = (0.5 * preact[OWN] * (1.0 + tanh_val[OWN])).astype(BF16)
    slope = 0.5 * (1.0 + tanh_val) + 0.5 * preact * (1.0 - tanh_val * tanh_val) * GELU_SCALE * (
        1.0 + 3.0 * square
    )
    hidden_out[...] = hidden
    scale = layer_scale[...]
    d_branch = cotan * scale
    d_branch_b = d_branch.astype(BF16)
    d_branch_out[...] = d_branch_b[OWN]
    d_pre = mm(d_branch_b, w_down[...], ((1,), (1,))) * slope
    d_pre_b = d_pre.astype(BF16)
    d_pre_out[...] = d_pre_b[OWN]
    d_lnout = mm(d_pre_b, w_up[...], ((1,), (1,)))
    e = d_lnout * gain
    d_spatial = inv_std * (
        e
        - jnp.mean(e, axis=1, keepdims=True)
        - standard * jnp.mean(e * standard, axis=1, keepdims=True)
    )
    d_out[...] = d_spatial
    branch = (mm(hidden, w_down[...]) + b_down[...]) * weight
    base = win[2 * HALO : 2 * HALO + HB, here, :].reshape(PIX_H, C)
    out = base + scale * branch
    output[...] = out.astype(BF16)
    if h == 0:
        edges[...] = jnp.zeros_like(edges)
        for r in range(ROWS_D):
            edges[6 * r : 6 * r + 6, :] = d_spatial[r * HALF : r * HALF + 6]
        for r in range(HB):
            at = LEFT_OUT + HALO * r
            edges[at : at + HALO, :] = out[r * HALF : r * HALF + HALO]
        send[...] = edges[...].astype(BF16)
    d_lnout = d_lnout[OWN]
    sums[0:1, :C] = rowsum(d_spatial[OWN])
    sums[1:2, :C] = rowsum(d_lnout * standard[OWN])
    sums[2:3, :C] = rowsum(d_lnout)
    sums[3:4, :C] = rowsum(d_branch[OWN])
    sums[4:5, :C] = rowsum(cotan[OWN] * branch)
    sums[5:6, :] = rowsum(d_pre[OWN])
    tap_sums[...] = jnp.zeros_like(tap_sums)
    for t in range(TILES_L):
        lanes = slice(128 * t, 128 * t + 128)
        d_rows = [
            d_spatial[(HALO + r) * HALF : (HALO + r + 1) * HALF, lanes] for r in range(HB)
        ]
        for dj in range(7):
            at = 2 + HALF * h + dj
            cols = eight_columns(win, range(HALO, HALO + ROWS_D), at, lanes)
            if h == 0 and dj != 3:
                mask = border_mask(is_first, dj, 0, HALF)
                cols = [col * mask for col in cols]
            for di in range(7):
                acc = cols[di] * d_rows[0]
                for r in range(1, HB):
                    acc = acc + cols[r + di] * d_rows[r]
                row = 56 * t + 7 * di + dj
                tap_sums[row : row + 1, :] = rowsum(acc)


def up_order():
    chan = np.arange(C).reshape(N_YL, N_X, N_C, N_Z // 2, 3).transpose(4, 2, 1, 0, 3).reshape(-1)
    return (np.arange(C)[:, None] == chan[None, :]).astype(np.float32)


def gradient_kernel(
    core, order, *refs
):
    halves = [refs[:6], refs[6:12]]
    mine, other, down, small = refs[12:]
    lnout, hidden, d_pre, d_branch = [
        jnp.concatenate([halves[0][i][...], halves[1][i][...]], axis=0) for i in range(4)
    ]
    is_zero = core[0] == 0

    def put(row, x, zero, one):
        size = zero.shape[0]
        mine[x, row : row + size, :] = jnp.where(is_zero, zero, one).astype(BF16)
        other[x, row : row + size, :] = jnp.where(is_zero, one, zero).astype(BF16)

    ordered = mm(lnout, order[...]).astype(BF16)
    ups = [mm(ordered[:, 128 * r : 128 * r + 128], d_pre, ((0,), (0,))) for r in range(3)]
    for q in range(4):
        for k, (r, t) in enumerate(UP_TILES[q]):
            for x in range(N_X):
                pair = [ups[r][64 * c + 16 * x : 64 * c + 16 * x + 16, 128 * t : 128 * t + 128] for c in range(2)]
                put((q * 8 + k) * 16, x, *pair)
    full = mm(hidden, d_branch, ((0,), (0,)))
    for t in range(TILES_L):
        down[t] = full[:, 128 * t : 128 * t + 128]
    for yh in range(2):
        for k, (s, t) in enumerate(DOWN_TILES[yh]):
            for x in range(N_X):
                for two in range(2):
                    pair = [
                        jnp.concatenate(
                            [
                                down[t, pl.ds(5 * (64 * yl + 16 * x + 8 * c) + s, 8, stride=5), :]
                                for yl in (2 * two, 2 * two + 1)
                            ],
                            axis=0,
                        )
                        for c in range(2)
                    ]
                    put(512 + (yh * 8 + k) * 32 + 16 * two, x, *pair)
    small[...] = jnp.zeros_like(small)
    small[:168, :] = halves[0][4][...] + halves[1][4][...]
    sums = halves[0][5][...] + halves[1][5][...]
    for i in range(5):
        for t in range(TILES_L):
            small[161 + 3 * i + t : 162 + 3 * i + t, :] = sums[i : i + 1, 128 * t : 128 * t + 128]
    for t in range(HID // 128):
        small[176 + t : 177 + t, :] = sums[5:6, 128 * t : 128 * t + 128]
    for x in range(N_X):
        pair = [
            jnp.concatenate([small[96 * c + 24 * x : 96 * c + 24 * x + 24], jnp.zeros((8, 128), F32)], axis=0)
            for c in range(2)
        ]
        put(1024, x, *pair)


def spread_kernel(part, after, out, total, buffer, done):
    total[...] = (
        (part[0].astype(F32) + part[1].astype(F32)) + (part[2].astype(F32) + part[3].astype(F32))
    )
    small = total[1024 : 1024 + SMALL, :]
    copies = []
    for yl in range(N_YL):
        for z in range(N_Z):
            for yh in range(N_YH):
                q = (z % 2) * 2 + yh
                up = total[pl.ds(q * 128 + yl * 4 + z // 2, 8, stride=16), :]
                down = total[pl.ds(512 + yh * 256 + yl * 8 + z, 8, stride=32), :]
                record = jnp.concatenate([up, down, small], axis=0)
                buffer[(yl * N_Z + z) * N_YH + yh] = record.astype(BF16)
        block = pl.ds(yl * N_Z * N_YH, N_Z * N_YH)
        copies.append(pltpu.make_async_copy(buffer.at[block], out.at[block], done.at[yl]))
        copies[-1].start()
    for copy in copies:
        copy.wait()


def gather_kernel(part, share, small):
    total = part[0].astype(F32)
    for i in range(1, N_YZ):
        total = total + part[i].astype(F32)
    share[...] = total[:16]
    for i in range(N_X * N_C):
        small[i] = total[16:]


def final_kernel(small, dw, *vectors):
    for t in range(TILES_L):
        dw[:, 128 * t : 128 * t + 128] = small[56 * t : 56 * t + 49, :]
    for i in range(5):
        for t in range(TILES_L):
            vectors[i][pl.ds(128 * t, 128)] = small[161 + 3 * i + t, :]
    for t in range(HID // 128):
        vectors[5][pl.ds(128 * t, 128)] = small[176 + t, :]


def finish_kernel(
    at_ends, after, d_left, d_right, out_left, out_right, got, cot, taps, grad, output, win
):
    halo = got[...].astype(F32)
    column = lax.broadcasted_iota(jnp.int32, (HALF, 1), 0)
    here = jnp.where((column < HALO) & (at_ends[0] > 0), 0.0, 1.0)
    beyond = lax.broadcasted_iota(jnp.int32, (6, 1), 0)
    there = jnp.where((beyond >= HALO) & (at_ends[1] > 0), 0.0, 1.0)
    for r in range(HB):
        at = LEFT_OUT + HALO * r
        win[r, 8 : 8 + HALF, :] = out_left[r * HALF : (r + 1) * HALF, :].astype(F32)
        win[r, 8 + HALF : 8 + WB, :] = out_right[r * HALF : (r + 1) * HALF, :].astype(F32)
        win[r, 8 + WB : 8 + WB + HALO, :] = halo[at : at + HALO]
    output[...] = win[:HB, 8 + HALO : 8 + HALO + WB, :].reshape(PIX, C).astype(BF16)
    for r in range(ROWS_D):
        win[r, 8 : 8 + HALF, :] = d_left[r * HALF : (r + 1) * HALF, :] * here
        win[r, 8 + HALF : 8 + WB, :] = d_right[r * HALF : (r + 1) * HALF, :]
        win[r, 8 + WB : 14 + WB, :] = halo[6 * r : 6 * r + 6] * there

    def start(r, h, lanes):
        return cot[r * WB : (r + 1) * WB, lanes].astype(F32)[HALF * h : HALF * h + HALF]

    def store(r, h, lanes, value):
        at = r * WB + HALF * h
        grad[at : at + HALF, lanes] = value

    depthwise(win, taps, HB, 8, (0, 1), start, True, store)


def core_sum_kernel(mine, got, send, out, send_out, buffer, done):
    copies = []
    for x in range(N_X):
        buffer[x] = (mine[x].astype(F32) + got[x].astype(F32)).astype(BF16)
        copies.append(pltpu.make_async_copy(buffer.at[x], out.at[x], done.at[x]))
        copies[-1].start()
    send_out[...] = send[...]
    for copy in copies:
        copy.wait()


def neighbours(before_edge, after_edge, axes):
    size = lax.axis_size(axes)
    up = [(i, i + 1) for i in range(size - 1)]
    down = [(i + 1, i) for i in range(size - 1)]
    return lax.ppermute(after_edge, axes, up), lax.ppermute(before_edge, axes, down)


def body(
    features, w_query, w_key, w_value, w_out, logit_scale, dw_kernel, dw_bias, ln_gain, ln_bias,
    w_up, b_up, w_down, b_down, layer_scale, cotangent, tile_list,
):
    row = lambda v: v.reshape(1, -1)
    flat = features.reshape(PIX, C)
    cot = cotangent.reshape(PIX, C)

    (copies,) = call(pool_kernel, [((N_ROW, WB, C), BF16)], features, nbytes=500_000)
    pooled = lax.all_to_all(copies, ROW, 0, 0, tiled=True).reshape(N_ROW * WB, C)

    shared = ((3 * HALO * WB, C), BF16)
    tiles = tile_list.reshape(-1)
    masked, feat_first, feat_last = call(
        prepare_kernel, [((PIX, C), BF16), shared, shared],
        tiles, copies, flat, cot, smem=(0,), fence=(1,), nbytes=800_000,
    )
    above, below = neighbours(feat_first, feat_last, ROW)
    (query,) = call(
        query_kernel, [((2, ROWS_M * WB // 2, C), BF16)], flat, above, below, w_query,
        flops=2 * 10**8, nbytes=900_000,
    )
    at_row = lax.axis_index(ROW)
    valid = jnp.stack([at_row > 0, at_row < N_ROW - 1]).astype(jnp.int32)
    inputs = (logit_scale, valid, pooled, query, flat, above, below, w_key, w_value, w_out)
    half_mixed = ((ROWS_M * HALF, C), BF16)
    cost = dict(flops=5 * 10**8, nbytes=1_500_000, trans=250_000)
    mixed_right, send = call(
        right_attention_kernel, [half_mixed, ((RIGHT, C), BF16)], *inputs, tiles, masked,
        scratch=[pltpu.VMEM((ROWS_D, WB, C), F32), pltpu.VMEM((RIGHT, C), F32)],
        smem=(0, 1, 10), **cost,
    )
    n_col = lax.axis_size(COL)
    at_col = lax.axis_index(COL)
    got = lax.ppermute(send, COL, [(i, (i + 1) % n_col) for i in range(n_col)])
    (mixed_left,) = call(
        left_attention_kernel, [half_mixed], *inputs, mixed_right, smem=(0, 1), fence=(10,), **cost
    )
    ends = jnp.stack([at_col == 0, at_col == n_col - 1]).astype(jnp.int32)

    half_outs = [
        ((PIX_H, C), BF16), ((ROWS_D * HALF, C), F32), ((PIX_H, C), BF16), ((PIX_H, HID), BF16),
        ((PIX_H, HID), BF16), ((PIX_H, C), BF16), ((8, HID), F32), ((168, 128), F32),
    ]
    half_scratch = [
        pltpu.VMEM((ROWS_M, WCOL, C), F32), pltpu.VMEM((ROWS_D, WCOL, C), F32),
        pltpu.VMEM((ROWS_D * HALF, C), F32),
    ]
    params = (
        dw_kernel, row(dw_bias), row(ln_gain), row(ln_bias), w_up, row(b_up), w_down, row(b_down),
        row(layer_scale),
    )
    cost = dict(flops=10**9, nbytes=4_000_000, trans=150_000)
    out_right, d_right, *stats_right, sums_right, taps_right = call(
        right_half_kernel, half_outs, tiles, mixed_left, mixed_right, masked, above, below, *params,
        scratch=half_scratch, smem=(0,), **cost,
    )
    out_left, d_left, *stats_left, sums_left, taps_left, send = call(
        left_half_kernel, half_outs + [((LEFT, C), BF16)],
        ends, tiles, mixed_left, mixed_right, got, masked, above, below, *params,
        scratch=half_scratch + [pltpu.VMEM((LEFT, C), F32)], smem=(0, 1), **cost,
    )

    core = lax.axis_index("c").reshape(1)
    order = jnp.asarray(up_order(), BF16)
    record = ((N_X, REC, 128), BF16)
    mine, other = call(
        gradient_kernel, [record, record],
        core, order, *stats_left, taps_left, sums_left, *stats_right, taps_right, sums_right,
        scratch=[
            pltpu.VMEM((TILES_L, HID, 128), F32),
            pltpu.VMEM((8 * SMALL, 128), F32),
        ],
        smem=(0,), flops=2 * 10**9, nbytes=4_000_000,
    )
    got = lax.ppermute(other, "c", [(0, 1), (1, 0)])
    part, send = call(
        core_sum_kernel, [record, ((LEFT, C), BF16)], mine, got, send, own=(0,), nbytes=3_000_000,
        scratch=[pltpu.VMEM((N_X, REC, 128), BF16), pltpu.SemaphoreType.DMA((N_X,))],
    )
    part = lax.all_to_all(part, "x", 0, 0, tiled=True)
    got = lax.ppermute(send, COL, [(i, (i - 1) % n_col) for i in range(n_col)])
    (spread,) = call(
        spread_kernel, [((N_YZ, 16 + SMALL, 128), BF16)], part, got, fence=(1,),
        scratch=[
            pltpu.VMEM((REC, 128), F32), pltpu.VMEM((N_YZ, 16 + SMALL, 128), BF16),
            pltpu.SemaphoreType.DMA((N_YL,)),
        ],
        own=(0,), nbytes=2_000_000,
    )
    part = lax.all_to_all(spread, YZ, 0, 0, tiled=True)
    share, small = call(
        gather_kernel, [((16, 128), F32), ((N_X * N_C, SMALL, 128), F32)], part, nbytes=800_000
    )
    small = lax.all_to_all(small, CX, 0, 0, tiled=True)
    vectors = call(
        final_kernel, [((49, C), F32)] + [((C,), F32)] * 5 + [((HID,), F32)],
        small.reshape(-1, 128), nbytes=200_000,
    )
    shares = share.reshape(2, 8 * 128)
    shares = jnp.where(lax.axis_index("yh") == 0, shares[:, :SHARE], shares[:, 8 * 128 - SHARE :])
    grad_mixed, output = call(
        finish_kernel, [((PIX, C), F32), ((PIX, C), BF16)],
        ends, spread, d_left, d_right, out_left, out_right, got, cot, dw_kernel,
        scratch=[pltpu.VMEM((ROWS_D, WCOL, C), F32)], smem=(0,), fence=(1,), flops=10**7, nbytes=1_000_000,
    )
    bias, gain, shift, b_down_grad, scale_grad, b_up_grad = vectors[1:]
    return (
        output.reshape(HB, WB, C), grad_mixed.reshape(HB, WB, C), shares[0], shares[1],
        vectors[0], bias, gain, shift, b_up_grad, b_down_grad, scale_grad,
    )


def solution(mesh):
    mesh = Mesh(mesh.devices.reshape(N_YL, N_X, N_C, N_Z, N_YH), ROW + COL)
    block = P(ROW, COL, None)
    in_specs = (block,) + (P(),) * 14 + (block, block)
    out_specs = (block, block, P(ROW + COL), P(ROW + COL)) + (P(),) * 7
    return jax.shard_map(body, mesh=mesh, in_specs=in_specs, out_specs=out_specs, check_vma=False)
```

```python
import numpy as np
import jax
import jax.numpy as jnp
from jax import lax
from jax.experimental import pallas as pl
from jax.experimental.pallas import tpu as pltpu
from jax.sharding import Mesh, PartitionSpec as P

ROW = ("yl", "x", "c")
COL = ("z", "yh")
YZ = ("yl", "z", "yh")
CX = ("c", "x")

F32 = jnp.float32
BF16 = jnp.bfloat16
EPS_NORM = 1e-06
GELU_SCALE = 0.7978845608028654
TS = 4
HB = 8
WB = 16
PIX = HB * WB
C = 384
HID = 1280
HEADS = 6
TILES_L = C // 128
N_YL, N_X, N_C, N_Z, N_YH = 4, 4, 2, 8, 2
N_ROW = N_YL * N_X * N_C
N_YZ = N_YL * N_Z * N_YH
SHARE = 960
SMALL = 24
REC = 1056
WCOL = 32
TILES = 8
HALO = 3
ROWS_M = HB + 4 * HALO
ROWS_D = HB + 2 * HALO
RIGHT_COT = 2 * HALO * ROWS_M
RIGHT_HIT = RIGHT_COT + HALO * ROWS_D
RIGHT = 176
LEFT_OUT = 2 * HALO * ROWS_D
LEFT = 112
HALF = WB // 2
PIX_H = HB * HALF
OWN = slice(HALO * HALF, HALO * HALF + PIX_H)

UP_TILES = (
    [(0, t) for t in range(8)],
    [(0, 7), (0, 8), (0, 9)] + [(1, t) for t in range(5)],
    [(1, t) for t in range(5, 10)] + [(2, t) for t in range(3)],
    [(2, t) for t in range(2, 10)],
)
DOWN_TILES = (
    [(0, t) for t in range(3)] + [(1, t) for t in range(3)] + [(2, 0), (2, 1)],
    [(2, 1), (2, 2)] + [(3, t) for t in range(3)] + [(4, t) for t in range(3)],
)


def call(
    kernel, outs, *args, scratch=(), smem=(), fence=(), hbm=(), own=(), flops=0, nbytes=0, trans=0, vmem=16
):
    n_in, n_out, n_scratch = len(args), len(outs), len(scratch)

    def run(*refs):
        targets = list(refs[n_in : n_in + n_out])
        extra = refs[n_in + n_out + n_scratch :]
        copies = []
        for j, i in enumerate(hbm):
            copies.append(pltpu.make_async_copy(extra[2 * j], targets[i], extra[2 * j + 1]))
            targets[i] = extra[2 * j]
        kernel(*refs[:n_in], *targets, *refs[n_in + n_out : n_in + n_out + n_scratch])
        for copy in copies:
            copy.start()
        for copy in copies:
            copy.wait()

    specs = [
        pl.BlockSpec(
            memory_space=pltpu.SMEM if i in smem else pl.ANY if i in fence else pltpu.VMEM
        )
        for i in range(n_in)
    ]
    buffers = [b for i in hbm for b in (pltpu.VMEM(*outs[i]), pltpu.SemaphoreType.DMA(()))]
    return pl.pallas_call(
        run,
        out_shape=[jax.ShapeDtypeStruct(s, d) for s, d in outs],
        in_specs=specs,
        out_specs=[
            pl.BlockSpec(memory_space=pltpu.HBM if i in hbm or i in own else pltpu.VMEM) for i in range(n_out)
        ],
        scratch_shapes=list(scratch) + buffers,
        compiler_params=pltpu.CompilerParams(vmem_limit_bytes=vmem * 1024 * 1024),
        cost_estimate=pl.CostEstimate(flops=flops, bytes_accessed=nbytes, transcendentals=trans),
    )(*args)


def mm(a, b, dims=((1,), (0,))):
    return lax.dot_general(a, b, (dims, ((), ())), preferred_element_type=F32)


def head_scaled(values):
    block = lax.broadcasted_iota(jnp.int32, (C, C), 0) // 64
    same = (block == lax.broadcasted_iota(jnp.int32, (C, C), 1) // 64).astype(F32).astype(BF16)
    squares = values * values
    high = squares.astype(BF16)
    low = (squares - high.astype(F32)).astype(BF16)
    return values * lax.rsqrt(mm(high, same) + mm(low, same) + EPS_NORM)


def pool_kernel(feat, out):
    total = feat[0].astype(F32)
    for r in range(1, HB):
        total = total + feat[r].astype(F32)
    mean = (total * (1.0 / HB)).astype(BF16)
    for i in range(N_ROW):
        out[i] = mean


def prepare_kernel(tiles, after, feat, cot, masked, first, last):
    pixel = lax.broadcasted_iota(jnp.int32, (PIX, 1), 0)
    value = (cot[...].astype(F32) * occupied(tiles, pixel // WB, pixel % WB)).astype(BF16)
    masked[...] = value
    n = 2 * HALO * WB
    m = HALO * WB
    first[:n, :] = feat[:n, :]
    first[n:, :] = value[:m]
    last[:n, :] = feat[PIX - n :, :]
    last[n:, :] = value[PIX - m :]


def occupied(tiles, row, col):
    tile = (row // TS) * (WB // TS) + col // TS
    weight = jnp.zeros(tile.shape, F32)
    for i in range(TILES):
        weight = jnp.where(tile == tiles[i], 1.0, weight)
    return weight


def split_columns(rows):
    shaped = rows.reshape(rows.shape[0] // WB, 2, WB // 2, rows.shape[1])
    return [shaped[:, h].reshape(-1, rows.shape[1]) for h in range(2)]


def stacked_rows(feat, above, below):
    n = 2 * HALO * WB
    return jnp.concatenate([above[:n, :], feat[...], below[:n, :]], axis=0)


def right_query_kernel(feat, above, below, w_query, out):
    out[...] = half_query(1, feat, above, below, w_query)


def left_query_kernel(feat, above, below, w_query, after, out):
    out[...] = half_query(0, feat, above, below, w_query)


def half_query(h, feat, above, below, w_query):
    rows = split_columns(stacked_rows(feat, above, below).astype(F32))[h].astype(BF16)
    return head_scaled(mm(rows, w_query[...])).astype(BF16)


def right_attention_kernel(
    scale, valid, pooled, query, feat, above, below, w_key, w_value, w_out, tiles, masked,
    mixed, send, cot_grid, edges,
):
    out = attention(1, scale, valid, pooled, query, feat, above, below, w_key, w_value, w_out)
    mixed[...] = out.astype(BF16)
    cot_grid[...] = cot_rows(masked, above, below).astype(F32).reshape(ROWS_D, WB, C)
    edges[...] = jnp.zeros_like(edges)
    for r in range(ROWS_M):
        edges[6 * r : 6 * r + 6, :] = out[HALF * r + HALF - 6 : HALF * r + HALF]
    for r in range(ROWS_D):
        at = RIGHT_COT + HALO * r
        edges[at : at + HALO, :] = cot_grid[r, WB - HALO :, :]
    tile_row = lax.broadcasted_iota(jnp.int32, (1, C), 1) // 128 * TS
    edges[RIGHT_HIT : RIGHT_HIT + 1, :] = occupied(tiles, tile_row, jnp.full((1, C), WB - 1))
    send[...] = edges[...].astype(BF16)


def left_attention_kernel(
    scale, valid, pooled, query, feat, above, below, w_key, w_value, w_out, after, mixed
):
    out = attention(0, scale, valid, pooled, query, feat, above, below, w_key, w_value, w_out)
    mixed[...] = out.astype(BF16)


def attention(h, scale, valid, pooled, query, feat, above, below, w_key, w_value, w_out):
    rows = split_columns(pooled[...].astype(F32))[h].astype(BF16)
    keys = head_scaled(mm(rows, w_key[...])).astype(BF16)
    values = mm(rows, w_value[...]).astype(BF16)
    half_feat = split_columns(stacked_rows(feat, above, below).astype(F32))[h]
    n_query, n_keys = ROWS_M * HALF, N_ROW * HALF
    same = (
        lax.broadcasted_iota(jnp.int32, (n_query, n_keys), 0) % HALF
        == lax.broadcasted_iota(jnp.int32, (n_query, n_keys), 1) % HALF
    )
    lower = lax.broadcasted_iota(jnp.int32, (n_query, 128), 1) < 64
    row = lax.broadcasted_iota(jnp.int32, (n_query, 1), 0) // HALF
    inside = ((row >= 2 * HALO) | (valid[0] > 0)) & ((row < 2 * HALO + HB) | (valid[1] > 0))
    pairs = []
    for pair in range(HEADS // 2):
        lanes = slice(128 * pair, 128 * pair + 128)
        q = query[:, lanes].astype(F32)
        parts = []
        for sub in range(2):
            q_half = jnp.where(lower if sub == 0 else ~lower, q, 0.0).astype(BF16)
            scores = mm(q_half, keys[:, lanes], ((1,), (1,)))
            weight = jnp.where(same, jnp.exp(scores * scale[2 * pair + sub]), 0.0)
            total = jnp.sum(weight, axis=1, keepdims=True)
            parts.append(mm(weight.astype(BF16), values[:, lanes]) / total)
        pairs.append(jnp.where(lower, parts[0], parts[1]).astype(BF16))
    attended = jnp.concatenate(pairs, axis=1)
    return jnp.where(inside, half_feat + mm(attended, w_out[...]), 0.0)


def cot_rows(masked, above, below):
    n = 2 * HALO * WB
    return jnp.concatenate([above[n:, :], masked[...], below[n:, :]], axis=0)


def border_mask(is_first, dj, start, size):
    u = lax.broadcasted_iota(jnp.int32, (size, 128), 0) + start
    crosses = (u < HALO) != (u + dj < 2 * HALO)
    return jnp.where(crosses & is_first, 0.0, 1.0)


def eight_columns(win, rows, at, lanes):
    shift = at % 8
    low = [win[r, at - shift : at - shift + 8, lanes] for r in rows]
    if shift == 0:
        return low
    sub = lax.broadcasted_iota(jnp.int32, (8, 128), 0)
    high = [win[r, at - shift + 8 : at - shift + 16, lanes] for r in rows]
    return [
        pltpu.roll(jnp.where(sub < shift, b, a), 8 - shift, axis=0) for a, b in zip(low, high)
    ]


def depthwise(win, taps, n_out, base, halves, start, flip, store, is_first=None):
    masks = [None] * 7
    if is_first is not None:
        masks = [border_mask(is_first, dj, 0, HALF) for dj in range(7)]
    for t in range(TILES_L):
        lanes = slice(128 * t, 128 * t + 128)
        for h in halves:
            acc = [start(r, h, lanes) for r in range(n_out)]
            for dj in range(7):
                at = base + HALF * h + dj
                cols = eight_columns(win, range(n_out + 6), at, lanes)
                if h == 0 and dj != 3 and is_first is not None:
                    cols = [col * masks[dj] for col in cols]
                for di in range(7):
                    tap = 7 * di + dj if not flip else 7 * (6 - di) + (6 - dj)
                    k = taps[tap : tap + 1, lanes]
                    for r in range(n_out):
                        acc[r] = acc[r] + cols[r + di] * k
            for r in range(n_out):
                store(r, h, lanes, acc[r])


def rowsum(a):
    return jnp.sum(a, axis=0, keepdims=True)


def right_half_kernel(tiles, mixed_left, mixed_right, masked, above, below, *refs):
    sublayer(1, None, tiles, mixed_left, mixed_right, None, masked, above, below, *refs)


def left_half_kernel(at_first, tiles, mixed_left, mixed_right, got, masked, above, below, *refs):
    sublayer(0, at_first, tiles, mixed_left, mixed_right, got, masked, above, below, *refs)


def sublayer(
    h, at_first, tiles, mixed_left, mixed_right, got, masked, above, below, taps, dw_bias, ln_gain,
    ln_bias, w_up, b_up, w_down, b_down, layer_scale, output, d_out, lnout_out, hidden_out,
    d_pre_out, d_branch_out, sums, tap_sums, *refs,
):
    is_first = None
    if h == 0:
        send, win, grid, spat, edges = refs
        is_first = at_first[0] > 0
        halo = got[...].astype(F32)
    else:
        win, grid, spat = refs
    for i, mixed in enumerate((mixed_left, mixed_right)):
        values = mixed[...].astype(F32)
        for r in range(ROWS_M):
            win[r, 8 + HALF * i : 8 + HALF * i + HALF, :] = values[r * HALF : (r + 1) * HALF]
    if h == 0:
        for r in range(ROWS_M):
            win[r, 2:8, :] = halo[6 * r : 6 * r + 6]
    grid[:, 8 : 8 + WB, :] = cot_rows(masked, above, below).astype(F32).reshape(ROWS_D, WB, C)
    pixel = lax.broadcasted_iota(jnp.int32, (PIX_H, 1), 0)
    row, col = pixel // HALF, pixel % HALF + HALF * h - HALO
    weight = occupied(tiles, row, jnp.maximum(col, 0))
    if h == 0:
        for r in range(ROWS_D):
            at = RIGHT_COT + HALO * r
            grid[r, 8 - HALO : 8, :] = halo[at : at + HALO]
        hits = halo[RIGHT_HIT : RIGHT_HIT + 1]
        before = jnp.where(row < TS, hits[:, 0:1], hits[:, 128:129])
        weight = jnp.where(col < 0, before, weight)
    here = slice(8 - HALO + HALF * h, 8 - HALO + HALF * h + HALF)
    cotan = grid[:, here, :].reshape(ROWS_D * HALF, C)

    def start(r, h, lanes):
        return jnp.broadcast_to(dw_bias[:, lanes], (HALF, 128))

    def store(r, h, lanes, value):
        spat[r * HALF : (r + 1) * HALF, lanes] = value

    depthwise(win, taps, ROWS_D, 2, (h,), start, False, store, is_first)
    spatial = spat[...]
    center = spatial - jnp.mean(spatial, axis=1, keepdims=True)
    inv_std = lax.rsqrt(jnp.mean(center * center, axis=1, keepdims=True) + EPS_NORM)
    standard = center * inv_std
    gain = ln_gain[...]
    lnout = (standard * gain + ln_bias[...]).astype(BF16)
    lnout_out[...] = lnout[OWN]
    preact = mm(lnout, w_up[...]) + b_up[...]
    square = 0.044715 * preact * preact
    tanh_val = jnp.tanh(GELU_SCALE * preact * (1.0 + square))
    hidden = (0.5 * preact[OWN] * (1.0 + tanh_val[OWN])).astype(BF16)
    slope = 0.5 * (1.0 + tanh_val) + 0.5 * preact * (1.0 - tanh_val * tanh_val) * GELU_SCALE * (
        1.0 + 3.0 * square
    )
    hidden_out[...] = hidden
    scale = layer_scale[...]
    d_branch = cotan * scale
    d_branch_b = d_branch.astype(BF16)
    d_branch_out[...] = d_branch_b[OWN]
    d_pre = mm(d_branch_b, w_down[...], ((1,), (1,))) * slope
    d_pre_b = d_pre.astype(BF16)
    d_pre_out[...] = d_pre_b[OWN]
    d_lnout = mm(d_pre_b, w_up[...], ((1,), (1,)))
    e = d_lnout * gain
    d_spatial = inv_std * (
        e
        - jnp.mean(e, axis=1, keepdims=True)
        - standard * jnp.mean(e * standard, axis=1, keepdims=True)
    )
    d_out[...] = d_spatial
    branch = (mm(hidden, w_down[...]) + b_down[...]) * weight
    base = win[2 * HALO : 2 * HALO + HB, here, :].reshape(PIX_H, C)
    out = base + scale * branch
    output[...] = out.astype(BF16)
    if h == 0:
        edges[...] = jnp.zeros_like(edges)
        for r in range(ROWS_D):
            edges[6 * r : 6 * r + 6, :] = d_spatial[r * HALF : r * HALF + 6]
        for r in range(HB):
            at = LEFT_OUT + HALO * r
            edges[at : at + HALO, :] = out[r * HALF : r * HALF + HALO]
        send[...] = edges[...].astype(BF16)
    d_lnout = d_lnout[OWN]
    sums[0:1, :C] = rowsum(d_spatial[OWN])
    sums[1:2, :C] = rowsum(d_lnout * standard[OWN])
    sums[2:3, :C] = rowsum(d_lnout)
    sums[3:4, :C] = rowsum(d_branch[OWN])
    sums[4:5, :C] = rowsum(cotan[OWN] * branch)
    sums[5:6, :] = rowsum(d_pre[OWN])
    tap_sums[...] = jnp.zeros_like(tap_sums)
    for t in range(TILES_L):
        lanes = slice(128 * t, 128 * t + 128)
        d_rows = [
            d_spatial[(HALO + r) * HALF : (HALO + r + 1) * HALF, lanes] for r in range(HB)
        ]
        for dj in range(7):
            at = 2 + HALF * h + dj
            cols = eight_columns(win, range(HALO, HALO + ROWS_D), at, lanes)
            if h == 0 and dj != 3:
                mask = border_mask(is_first, dj, 0, HALF)
                cols = [col * mask for col in cols]
            for di in range(7):
                acc = cols[di] * d_rows[0]
                for r in range(1, HB):
                    acc = acc + cols[r + di] * d_rows[r]
                row = 56 * t + 7 * di + dj
                tap_sums[row : row + 1, :] = rowsum(acc)


def up_order():
    chan = np.arange(C).reshape(N_YL, N_X, N_C, N_Z // 2, 3).transpose(4, 2, 1, 0, 3).reshape(-1)
    return (np.arange(C)[:, None] == chan[None, :]).astype(np.float32)


def gradient_kernel(
    core, order, *refs
):
    halves = [refs[:6], refs[6:12]]
    mine, other, down, small = refs[12:]
    lnout, hidden, d_pre, d_branch = [
        jnp.concatenate([halves[0][i][...], halves[1][i][...]], axis=0) for i in range(4)
    ]
    is_zero = core[0] == 0

    def put(row, x, zero, one):
        size = zero.shape[0]
        mine[x, row : row + size, :] = jnp.where(is_zero, zero, one).astype(BF16)
        other[x, row : row + size, :] = jnp.where(is_zero, one, zero).astype(BF16)

    ordered = mm(lnout, order[...]).astype(BF16)
    ups = [mm(ordered[:, 128 * r : 128 * r + 128], d_pre, ((0,), (0,))) for r in range(3)]
    for q in range(4):
        for k, (r, t) in enumerate(UP_TILES[q]):
            for x in range(N_X):
                pair = [ups[r][64 * c + 16 * x : 64 * c + 16 * x + 16, 128 * t : 128 * t + 128] for c in range(2)]
                put((q * 8 + k) * 16, x, *pair)
    full = mm(hidden, d_branch, ((0,), (0,)))
    for t in range(TILES_L):
        down[t] = full[:, 128 * t : 128 * t + 128]
    for yh in range(2):
        for k, (s, t) in enumerate(DOWN_TILES[yh]):
            for x in range(N_X):
                for two in range(2):
                    pair = [
                        jnp.concatenate(
                            [
                                down[t, pl.ds(5 * (64 * yl + 16 * x + 8 * c) + s, 8, stride=5), :]
                                for yl in (2 * two, 2 * two + 1)
                            ],
                            axis=0,
                        )
                        for c in range(2)
                    ]
                    put(512 + (yh * 8 + k) * 32 + 16 * two, x, *pair)
    small[...] = jnp.zeros_like(small)
    small[:168, :] = halves[0][4][...] + halves[1][4][...]
    sums = halves[0][5][...] + halves[1][5][...]
    for i in range(5):
        for t in range(TILES_L):
            small[161 + 3 * i + t : 162 + 3 * i + t, :] = sums[i : i + 1, 128 * t : 128 * t + 128]
    for t in range(HID // 128):
        small[176 + t : 177 + t, :] = sums[5:6, 128 * t : 128 * t + 128]
    for x in range(N_X):
        pair = [
            jnp.concatenate([small[96 * c + 24 * x : 96 * c + 24 * x + 24], jnp.zeros((8, 128), F32)], axis=0)
            for c in range(2)
        ]
        put(1024, x, *pair)


def spread_kernel(part, after, out, total, buffer, done):
    total[...] = (
        (part[0].astype(F32) + part[1].astype(F32)) + (part[2].astype(F32) + part[3].astype(F32))
    )
    small = total[1024 : 1024 + SMALL, :]
    copies = []
    for yl in range(N_YL):
        for z in range(N_Z):
            for yh in range(N_YH):
                q = (z % 2) * 2 + yh
                up = total[pl.ds(q * 128 + yl * 4 + z // 2, 8, stride=16), :]
                down = total[pl.ds(512 + yh * 256 + yl * 8 + z, 8, stride=32), :]
                record = jnp.concatenate([up, down, small], axis=0)
                buffer[(yl * N_Z + z) * N_YH + yh] = record.astype(BF16)
        block = pl.ds(yl * N_Z * N_YH, N_Z * N_YH)
        copies.append(pltpu.make_async_copy(buffer.at[block], out.at[block], done.at[yl]))
        copies[-1].start()
    for copy in copies:
        copy.wait()


def gather_kernel(part, share, small):
    total = part[0].astype(F32)
    for i in range(1, N_YZ):
        total = total + part[i].astype(F32)
    share[...] = total[:16]
    for i in range(N_X * N_C):
        small[i] = total[16:]


def final_kernel(small, dw, *vectors):
    for t in range(TILES_L):
        dw[:, 128 * t : 128 * t + 128] = small[56 * t : 56 * t + 49, :]
    for i in range(5):
        for t in range(TILES_L):
            vectors[i][pl.ds(128 * t, 128)] = small[161 + 3 * i + t, :]
    for t in range(HID // 128):
        vectors[5][pl.ds(128 * t, 128)] = small[176 + t, :]


def finish_kernel(
    at_ends, after, d_left, d_right, out_left, out_right, got, cot, taps, grad, output, win
):
    halo = got[...].astype(F32)
    column = lax.broadcasted_iota(jnp.int32, (HALF, 1), 0)
    here = jnp.where((column < HALO) & (at_ends[0] > 0), 0.0, 1.0)
    beyond = lax.broadcasted_iota(jnp.int32, (6, 1), 0)
    there = jnp.where((beyond >= HALO) & (at_ends[1] > 0), 0.0, 1.0)
    for r in range(HB):
        at = LEFT_OUT + HALO * r
        win[r, 8 : 8 + HALF, :] = out_left[r * HALF : (r + 1) * HALF, :].astype(F32)
        win[r, 8 + HALF : 8 + WB, :] = out_right[r * HALF : (r + 1) * HALF, :].astype(F32)
        win[r, 8 + WB : 8 + WB + HALO, :] = halo[at : at + HALO]
    output[...] = win[:HB, 8 + HALO : 8 + HALO + WB, :].reshape(PIX, C).astype(BF16)
    for r in range(ROWS_D):
        win[r, 8 : 8 + HALF, :] = d_left[r * HALF : (r + 1) * HALF, :] * here
        win[r, 8 + HALF : 8 + WB, :] = d_right[r * HALF : (r + 1) * HALF, :]
        win[r, 8 + WB : 14 + WB, :] = halo[6 * r : 6 * r + 6] * there

    def start(r, h, lanes):
        return cot[r * WB : (r + 1) * WB, lanes].astype(F32)[HALF * h : HALF * h + HALF]

    def store(r, h, lanes, value):
        at = r * WB + HALF * h
        grad[at : at + HALF, lanes] = value

    depthwise(win, taps, HB, 8, (0, 1), start, True, store)


def core_sum_kernel(mine, got, send, out, send_out, buffer, done):
    copies = []
    for x in range(N_X):
        buffer[x] = (mine[x].astype(F32) + got[x].astype(F32)).astype(BF16)
        copies.append(pltpu.make_async_copy(buffer.at[x], out.at[x], done.at[x]))
        copies[-1].start()
    send_out[...] = send[...]
    for copy in copies:
        copy.wait()


def neighbours(before_edge, after_edge, axes):
    size = lax.axis_size(axes)
    up = [(i, i + 1) for i in range(size - 1)]
    down = [(i + 1, i) for i in range(size - 1)]
    return lax.ppermute(after_edge, axes, up), lax.ppermute(before_edge, axes, down)


def body(
    features, w_query, w_key, w_value, w_out, logit_scale, dw_kernel, dw_bias, ln_gain, ln_bias,
    w_up, b_up, w_down, b_down, layer_scale, cotangent, tile_list,
):
    row = lambda v: v.reshape(1, -1)
    flat = features.reshape(PIX, C)
    cot = cotangent.reshape(PIX, C)

    (copies,) = call(pool_kernel, [((N_ROW, WB, C), BF16)], features, nbytes=500_000)
    pooled = lax.all_to_all(copies, ROW, 0, 0, tiled=True).reshape(N_ROW * WB, C)

    shared = ((3 * HALO * WB, C), BF16)
    tiles = tile_list.reshape(-1)
    masked, feat_first, feat_last = call(
        prepare_kernel, [((PIX, C), BF16), shared, shared],
        tiles, copies, flat, cot, smem=(0,), fence=(1,), nbytes=800_000,
    )
    above, below = neighbours(feat_first, feat_last, ROW)
    half_mixed = ((ROWS_M * HALF, C), BF16)
    (query,) = call(
        right_query_kernel, [half_mixed], flat, above, below, w_query, flops=10**8, nbytes=900_000
    )
    at_row = lax.axis_index(ROW)
    valid = jnp.stack([at_row > 0, at_row < N_ROW - 1]).astype(jnp.int32)
    inputs = (logit_scale, valid, pooled, query, flat, above, below, w_key, w_value, w_out)
    cost = dict(flops=5 * 10**8, nbytes=1_500_000, trans=250_000)
    mixed_right, send = call(
        right_attention_kernel, [half_mixed, ((RIGHT, C), BF16)], *inputs, tiles, masked,
        scratch=[pltpu.VMEM((ROWS_D, WB, C), F32), pltpu.VMEM((RIGHT, C), F32)],
        smem=(0, 1, 10), **cost,
    )
    n_col = lax.axis_size(COL)
    at_col = lax.axis_index(COL)
    got = lax.ppermute(send, COL, [(i, (i + 1) % n_col) for i in range(n_col)])
    (query,) = call(
        left_query_kernel, [half_mixed], flat, above, below, w_query, mixed_right, fence=(4,),
        flops=10**8, nbytes=900_000,
    )
    inputs = inputs[:3] + (query,) + inputs[4:]
    (mixed_left,) = call(
        left_attention_kernel, [half_mixed], *inputs, mixed_right, smem=(0, 1), fence=(10,), **cost
    )
    ends = jnp.stack([at_col == 0, at_col == n_col - 1]).astype(jnp.int32)

    half_outs = [
        ((PIX_H, C), BF16), ((ROWS_D * HALF, C), F32), ((PIX_H, C), BF16), ((PIX_H, HID), BF16),
        ((PIX_H, HID), BF16), ((PIX_H, C), BF16), ((8, HID), F32), ((168, 128), F32),
    ]
    half_scratch = [
        pltpu.VMEM((ROWS_M, WCOL, C), F32), pltpu.VMEM((ROWS_D, WCOL, C), F32),
        pltpu.VMEM((ROWS_D * HALF, C), F32),
    ]
    params = (
        dw_kernel, row(dw_bias), row(ln_gain), row(ln_bias), w_up, row(b_up), w_down, row(b_down),
        row(layer_scale),
    )
    cost = dict(flops=10**9, nbytes=4_000_000, trans=150_000)
    out_right, d_right, *stats_right, sums_right, taps_right = call(
        right_half_kernel, half_outs, tiles, mixed_left, mixed_right, masked, above, below, *params,
        scratch=half_scratch, smem=(0,), **cost,
    )
    out_left, d_left, *stats_left, sums_left, taps_left, send = call(
        left_half_kernel, half_outs + [((LEFT, C), BF16)],
        ends, tiles, mixed_left, mixed_right, got, masked, above, below, *params,
        scratch=half_scratch + [pltpu.VMEM((LEFT, C), F32)], smem=(0, 1), **cost,
    )

    core = lax.axis_index("c").reshape(1)
    order = jnp.asarray(up_order(), BF16)
    record = ((N_X, REC, 128), BF16)
    mine, other = call(
        gradient_kernel, [record, record],
        core, order, *stats_left, taps_left, sums_left, *stats_right, taps_right, sums_right,
        scratch=[
            pltpu.VMEM((TILES_L, HID, 128), F32),
            pltpu.VMEM((8 * SMALL, 128), F32),
        ],
        smem=(0,), flops=2 * 10**9, nbytes=4_000_000,
    )
    got = lax.ppermute(other, "c", [(0, 1), (1, 0)])
    part, send = call(
        core_sum_kernel, [record, ((LEFT, C), BF16)], mine, got, send, own=(0,), nbytes=3_000_000,
        scratch=[pltpu.VMEM((N_X, REC, 128), BF16), pltpu.SemaphoreType.DMA((N_X,))],
    )
    part = lax.all_to_all(part, "x", 0, 0, tiled=True)
    got = lax.ppermute(send, COL, [(i, (i - 1) % n_col) for i in range(n_col)])
    (spread,) = call(
        spread_kernel, [((N_YZ, 16 + SMALL, 128), BF16)], part, got, fence=(1,),
        scratch=[
            pltpu.VMEM((REC, 128), F32), pltpu.VMEM((N_YZ, 16 + SMALL, 128), BF16),
            pltpu.SemaphoreType.DMA((N_YL,)),
        ],
        own=(0,), nbytes=2_000_000,
    )
    part = lax.all_to_all(spread, YZ, 0, 0, tiled=True)
    share, small = call(
        gather_kernel, [((16, 128), F32), ((N_X * N_C, SMALL, 128), F32)], part, nbytes=800_000
    )
    small = lax.all_to_all(small, CX, 0, 0, tiled=True)
    vectors = call(
        final_kernel, [((49, C), F32)] + [((C,), F32)] * 5 + [((HID,), F32)],
        small.reshape(-1, 128), nbytes=200_000,
    )
    shares = share.reshape(2, 8 * 128)
    shares = jnp.where(lax.axis_index("yh") == 0, shares[:, :SHARE], shares[:, 8 * 128 - SHARE :])
    grad_mixed, output = call(
        finish_kernel, [((PIX, C), F32), ((PIX, C), BF16)],
        ends, spread, d_left, d_right, out_left, out_right, got, cot, dw_kernel,
        scratch=[pltpu.VMEM((ROWS_D, WCOL, C), F32)], smem=(0,), fence=(1,), flops=10**7, nbytes=1_000_000,
    )
    bias, gain, shift, b_down_grad, scale_grad, b_up_grad = vectors[1:]
    return (
        output.reshape(HB, WB, C), grad_mixed.reshape(HB, WB, C), shares[0], shares[1],
        vectors[0], bias, gain, shift, b_up_grad, b_down_grad, scale_grad,
    )


def solution(mesh):
    mesh = Mesh(mesh.devices.reshape(N_YL, N_X, N_C, N_Z, N_YH), ROW + COL)
    block = P(ROW, COL, None)
    in_specs = (block,) + (P(),) * 14 + (block, block)
    out_specs = (block, block, P(ROW + COL), P(ROW + COL)) + (P(),) * 7
    return jax.shard_map(body, mesh=mesh, in_specs=in_specs, out_specs=out_specs, check_vma=False)
```
